256 devices in a mesh: seq: 64 (over z, y_lo, x), dp: 4 (over y_hi, core).
Axes of the slice: x: 4, y: 4 (y_hi: 2, y_lo: 2; y = y_hi * 2 + y_lo), z: 8, core: 2. Of those that a mesh axis runs over, the one named last changes fastest.
Arguments:
- queries: bfloat16 [32768, 8192], P(('dp', 'seq')), parts along dimension 0, may hold values from -6 to 6
- keys: bfloat16 [32768, 1024], P(('dp', 'seq')), parts along dimension 0, may hold values from -6 to 6
- values: bfloat16 [32768, 1024], P(('dp', 'seq')), parts along dimension 0, may hold values from -6 to 6
- outputs: bfloat16 [32768, 8192], P(('dp', 'seq')), parts along dimension 0, may hold values from -6 to 6
- out_grad: bfloat16 [32768, 8192], P(('dp', 'seq')), parts along dimension 0, may hold values from -6 to 6
- lse: float32 [64, 32768], P(None, ('dp', 'seq')), parts along dimension 1, may hold values from 3 to 7
- segments: int32 [32768], P(('dp', 'seq')), parts along dimension 0, may hold values from 0 to 127, never falling along the last dimension, each value on 1 to 2048 neighbouring positions
Outputs:
- grad_queries: bfloat16 [32768, 8192], P(('dp', 'seq')), parts along dimension 0
- grad_keys: bfloat16 [32768, 1024], P(('dp', 'seq')), parts along dimension 0
- grad_values: bfloat16 [32768, 1024], P(('dp', 'seq')), parts along dimension 0
The draws below stay inside these ranges and needn't reach their ends.
There are 4 independent parts, one for each index of `dp`. The reference program is written for one: setup_inputs(seed, part) draws one part's arguments, and reference() takes and returns one part's arrays. A program takes and returns all parts, laid end to end along the dimension named above; each array names one. Nothing has to cross between parts.
Inputs may be any that keep to these rules, and one draw needn't show every extreme that they name: `segments`: document ids never fall along the sequence; each document holds 1 to 2048 positions and one holds exactly 2048.
All inputs are finite; a program needn't handle non-finite values.
Results may differ from the reference program's by a relative error of at most 0.0055.
Values may be sent and summed in bfloat16 or wider, within the bound.
A program may use at most 128 MiB of HBM per device.

```python
import math
import jax
import jax.numpy as jnp
import numpy as np
from jax import lax

HEADS = 64
KV_HEADS = 8
HEAD_DIM = 128
TOKENS = 8192
QB = 512
DOC_MAX = 2048
COUNT = 128


def shard_levels(key, shape, split, least, largest):
    def one(axis_at, blocks):
        steps = jax.random.uniform(jax.random.fold_in(jax.random.fold_in(key, 6), axis_at), (blocks,), jnp.float32, least / len(split), largest / len(split))
        return jnp.repeat(jnp.exp(steps), shape[axis_at] // blocks).reshape((-1,) + (1,) * (len(shape) - axis_at - 1))

    loudness = one(*split[0])
    for cut in split[1:]:
        loudness = loudness * one(*cut)
    return loudness


def length_profile(number_of, total, most, lean):
    weights = [(1 << 20) // math.isqrt(standing ** lean) + 1 for standing in range(2, number_of + 1)]
    surplus, holding = total - most - (number_of - 1), [1] * (number_of - 1)
    while surplus > 0:
        candidates = [i for i in range(number_of - 1) if holding[i] < most]
        mass, left = sum([weights[i] for i in candidates]), surplus
        for i in candidates:
            extra = min(most - holding[i], max(1, left * weights[i] // mass), surplus)
            holding[i] = holding[i] + extra
            surplus = surplus - extra
    return np.array([most] + holding)


def uneven_parts(key, number_of, total, most, skew):
    if number_of == 2:
        one = jax.random.randint(key, (), max(1, total - most), min(most, total - 1) + 1)
        return jnp.stack([one, total - one])
    lengths = jnp.asarray(length_profile(number_of, total, most, skew), jnp.int32)
    pairs = (number_of - 1) // 2
    giver, receiver = lengths[1:1 + 2 * pairs:2], lengths[2:2 + 2 * pairs:2]
    slack = jnp.minimum(giver - 1, most - receiver)
    moved = jax.random.randint(jax.random.fold_in(key, 1), (pairs,), 0, 1 << 20) % (slack + 1)
    lengths = lengths.at[1:1 + 2 * pairs:2].set(giver - moved).at[2:2 + 2 * pairs:2].set(receiver + moved)
    return lengths[jax.random.permutation(jax.random.fold_in(key, 2), number_of)]


def centred(rng, shape, spread, limit, pieces=(), kind=jnp.bfloat16):
    entries = jax.random.normal(rng, shape, jnp.float32) * spread
    if len(pieces) > 0:
        entries = shard_levels(rng, shape, pieces, -0.22, 0.18) * entries
    return jnp.clip(entries, min=-limit, max=limit).astype(kind)


def setup_inputs(seed: int = 0, part: int = 0) -> dict:
    splits = jax.random.split(jax.random.key(seed), 8)
    part_keys = jax.random.split(jax.random.fold_in(splits[7], part), 8)
    return {
        "queries": centred(part_keys[0], (TOKENS, HEADS * HEAD_DIM), 1.0, 6.0, ((0, 64),)),
        "keys": centred(part_keys[1], (TOKENS, KV_HEADS * HEAD_DIM), 1.0, 6.0, ((0, 64),)),
        "values": centred(part_keys[2], (TOKENS, KV_HEADS * HEAD_DIM), 1.0, 6.0, ((0, 64),)),
        "outputs": centred(part_keys[3], (TOKENS, HEADS * HEAD_DIM), 1.0, 6.0, ((0, 64),)),
        "out_grad": centred(part_keys[4], (TOKENS, HEADS * HEAD_DIM), 1.0, 6.0, ((0, 64),)),
        "lse": jnp.clip(3.0 + 4.0 * jax.random.uniform(part_keys[5], (HEADS, TOKENS), jnp.float32) ** shard_levels(part_keys[5], (HEADS, TOKENS), ((1, 64),), -0.2, 0.2), 3.0, 7.0),
        "segments": jnp.searchsorted(jnp.cumsum(uneven_parts(part_keys[6], COUNT, TOKENS, DOC_MAX, 2)), jnp.arange(TOKENS), side="right").astype(jnp.int32),
    }


def widen(value):
    return lax.optimization_barrier(value.astype(jnp.bfloat16)).astype(jnp.float32)

def group_grads(q_heads, g_heads, k_cols_all, v_cols_all, lse_rows, delta_rows, seg_ids):
    length = seg_ids.shape[0]
    inv_root = 1.0 / math.sqrt(HEAD_DIM)
    block_rows = QB
    head_count = q_heads.shape[0]
    positions = jnp.arange(length, dtype=jnp.int32)

    def query_block(carried, block_index):
        row_start = (block_index * block_rows).astype(jnp.int32)
        q_rows = lax.dynamic_slice_in_dim(q_heads, row_start, block_rows, 1)
        g_rows = lax.dynamic_slice_in_dim(g_heads, row_start, block_rows, 1)
        lse_part = lax.dynamic_slice_in_dim(lse_rows, row_start, block_rows, 1)
        delta_part = lax.dynamic_slice_in_dim(delta_rows, row_start, block_rows, 1)
        seg_rows = lax.dynamic_slice_in_dim(seg_ids, row_start, block_rows, 0)
        pos_rows = lax.dynamic_slice_in_dim(positions, row_start, block_rows, 0)
        doc_first = jnp.min(jnp.where(seg_ids == seg_rows[0], positions, length))

        def tile_step(tile_index, loop_state):
            dq_block, dk_cols, dv_cols = loop_state
            col_start = (tile_index * block_rows).astype(jnp.int32)
            k_cols = lax.dynamic_slice_in_dim(k_cols_all, col_start, block_rows, 1)
            v_cols = lax.dynamic_slice_in_dim(v_cols_all, col_start, block_rows, 1)
            seg_cols = lax.dynamic_slice_in_dim(seg_ids, col_start, block_rows, 0)
            pos_cols = lax.dynamic_slice_in_dim(positions, col_start, block_rows, 0)
            scores = jnp.einsum('hqd,dk->hqk', q_rows, k_cols) * inv_root
            visible = (seg_rows[:, None] == seg_cols[None, :]) & (pos_cols[None, :] <= pos_rows[:, None])
            weights = jnp.where(visible[None], jnp.exp(scores - lse_part[:, :, None]), 0.0)
            d_weights = jnp.einsum('hqd,dk->hqk', g_rows, v_cols)
            dscore = widen(weights * (d_weights - delta_part[:, :, None]))
            weights_low = widen(weights)
            dq_block = dq_block + inv_root * jnp.einsum('hqk,dk->hqd', dscore, k_cols)
            dk_tile = inv_root * jnp.einsum('hqd,hqk->dk', q_rows, dscore)
            dv_tile = jnp.einsum('hqd,hqk->dk', g_rows, weights_low)
            dk_cols = lax.dynamic_update_slice_in_dim(dk_cols, lax.dynamic_slice_in_dim(dk_cols, col_start, block_rows, 1) + dk_tile, col_start, 1)
            dv_cols = lax.dynamic_update_slice_in_dim(dv_cols, lax.dynamic_slice_in_dim(dv_cols, col_start, block_rows, 1) + dv_tile, col_start, 1)
            return (dq_block, dk_cols, dv_cols)
        start_state = (jnp.zeros((head_count, block_rows, HEAD_DIM), jnp.float32), carried[0], carried[1])
        loop_state = lax.fori_loop(doc_first // block_rows, block_index + 1, tile_step, start_state)
        return ((loop_state[1], loop_state[2]), loop_state[0].astype(jnp.bfloat16))
    zero_cols = jnp.zeros((HEAD_DIM, length), jnp.float32)
    block_ids = jnp.arange(length // block_rows, dtype=jnp.int32)
    (dk_cols, dv_cols), dq_blocks = lax.scan(query_block, (zero_cols, zero_cols), block_ids)
    return (dq_blocks, dk_cols, dv_cols)

def reference(queries, keys, values, outputs, out_grad, lse, segments):
    group_size = HEADS // KV_HEADS
    q_all = queries.astype(jnp.float32).reshape(TOKENS, HEADS, HEAD_DIM).transpose(1, 0, 2)
    g_all = out_grad.astype(jnp.float32).reshape(TOKENS, HEADS, HEAD_DIM).transpose(1, 0, 2)
    o_all = outputs.astype(jnp.float32).reshape(TOKENS, HEADS, HEAD_DIM).transpose(1, 0, 2)
    delta = lax.optimization_barrier(jnp.sum(o_all * g_all, axis=2))
    dq_list = []
    dk_list = []
    dv_list = []
    for group_index in range(KV_HEADS):
        low_head = group_index * group_size
        high_head = low_head + group_size
        k_cols_all = keys[:, group_index * HEAD_DIM:(group_index + 1) * HEAD_DIM].astype(jnp.float32).T
        v_cols_all = values[:, group_index * HEAD_DIM:(group_index + 1) * HEAD_DIM].astype(jnp.float32).T
        dq_blocks, dk_cols, dv_cols = group_grads(q_all[low_head:high_head], g_all[low_head:high_head], k_cols_all, v_cols_all, lse[low_head:high_head], delta[low_head:high_head], segments)
        dq_list.append(dq_blocks.transpose(0, 2, 1, 3).reshape(TOKENS, group_size * HEAD_DIM))
        dk_list.append(dk_cols.T.astype(jnp.bfloat16))
        dv_list.append(dv_cols.T.astype(jnp.bfloat16))
    return (jnp.concatenate(dq_list, axis=1), jnp.concatenate(dk_list, axis=1), jnp.concatenate(dv_list, axis=1))
```

```python
import functools
import math

import jax
import jax.numpy as jnp
from jax import lax
from jax.experimental import pallas as pl
from jax.experimental.pallas import tpu as pltpu
from jax.sharding import PartitionSpec as P

D = 128
LOG2E = math.log2(math.e)
MESH = pl.DeviceIdType.MESH
PLANE = 8
HALO = 2
BLOCK = 256


def dev(index):
    return {"seq": index}


def greet(me, plane, rank, planes):
    barrier = pltpu.get_barrier_semaphore()
    for o in range(1, PLANE):
        peer = plane * PLANE + lax.rem(rank + o, PLANE)
        pl.semaphore_signal(barrier, inc=1, device_id=dev(peer), device_id_type=MESH)
    count = PLANE - 1
    for dz in range(1, HALO + 1):
        up = plane + dz < planes
        down = plane >= dz

        @pl.when(up)
        def _():
            pl.semaphore_signal(barrier, inc=1, device_id=dev(me + dz * PLANE), device_id_type=MESH)

        @pl.when(down)
        def _():
            pl.semaphore_signal(barrier, inc=1, device_id=dev(me - dz * PLANE), device_id_type=MESH)

        count = count + up.astype(jnp.int32) + down.astype(jnp.int32)
    pl.semaphore_wait(barrier, count)


def gather_kernel(
    planes, q, g, k, v, lse, delta, seg, q_all, g_all, k_win, v_win, lse_all, delta_all, seg_win,
    send, recv, z_send, z_recv, local,
):
    rows = q.shape[0]
    span = rows * PLANE
    wide = q_all.shape[1]
    heads = lse_all.shape[0]
    me = lax.axis_index("seq")
    plane, rank = me // PLANE, lax.rem(me, PLANE)

    def cols(index, width):
        return pl.ds(pl.multiple_of(index * width, width), width)

    own = HALO * span

    pieces = [
        (lambda p: seg, lambda s: seg_win.at[:, pl.ds(pl.multiple_of(own + s * rows, rows), rows)]),
        (lambda p: k.at[:, cols(p, D)], lambda s: k_win.at[pl.ds(pl.multiple_of(own + s * rows, rows), rows), :]),
        (lambda p: v.at[:, cols(p, D)], lambda s: v_win.at[pl.ds(pl.multiple_of(own + s * rows, rows), rows), :]),
        (lambda p: lse.at[cols(p, heads), :], lambda s: lse_all.at[:, cols(s, rows)]),
        (lambda p: delta.at[cols(p, heads), :], lambda s: delta_all.at[:, cols(s, rows)]),
        (lambda p: q.at[:, cols(p, wide)], lambda s: q_all.at[cols(s, rows), :]),
        (lambda p: g.at[:, cols(p, wide)], lambda s: g_all.at[cols(s, rows), :]),
    ]

    def own_copy(n):
        source, target = pieces[n]
        return pltpu.make_async_copy(source(rank), target(rank), local.at[n])

    def plane_copy(n, o):
        source, target = pieces[n]
        peer = lax.rem(rank + o, PLANE)
        return pltpu.make_async_remote_copy(
            source(peer), target(rank), send.at[n, o - 1], recv.at[n, o - 1],
            device_id=dev(plane * PLANE + peer), device_id_type=MESH,
        )

    def arrival(n, o):
        source, target = pieces[n]
        origin = lax.rem(rank + PLANE - o, PLANE)
        return pltpu.make_async_remote_copy(
            source(rank), target(origin), send.at[n, o - 1], recv.at[n, o - 1],
            device_id=dev(plane * PLANE + origin), device_id_type=MESH,
        )

    def z_copy(n, dz):
        if n == 0:
            whole = seg_win.at[:, pl.ds(own, span)]
            there = seg_win.at[:, pl.ds(own - dz * span, span)]
        else:
            win = (k_win, v_win)[n - 1]
            whole = win.at[pl.ds(own, span), :]
            there = win.at[pl.ds(own - dz * span, span), :]
        return pltpu.make_async_remote_copy(
            whole, there, z_send.at[n, dz - 1], z_recv.at[n, dz - 1],
            device_id=dev(me + dz * PLANE), device_id_type=MESH,
        )

    greet(me, plane, rank, planes)
    for n in range(len(pieces)):
        for o in range(1, PLANE):
            plane_copy(n, o).start()
        own_copy(n).start()
    for n in range(3):
        own_copy(n).wait()
        for o in range(1, PLANE):
            arrival(n, o).wait_recv()
        for dz in range(1, HALO + 1):
            @pl.when(plane + dz < planes)
            def _():
                z_copy(n, dz).start()
    for n in range(3, len(pieces)):
        own_copy(n).wait()
        for o in range(1, PLANE):
            arrival(n, o).wait_recv()
    for n in range(len(pieces)):
        for o in range(1, PLANE):
            plane_copy(n, o).wait_send()
    for n in range(3):
        for dz in range(1, HALO + 1):
            @pl.when(plane + dz < planes)
            def _():
                z_copy(n, dz).wait_send()

            @pl.when(plane >= dz)
            def _():
                z_copy(n, dz).wait_recv()


def gather(q, g, k, v, lse, delta, seg, planes):
    rows = q.shape[0]
    span = rows * PLANE
    heads = lse.shape[0] // PLANE
    window = (HALO + 1) * span
    any_space = pl.BlockSpec(memory_space=pl.ANY)
    return pl.pallas_call(
        functools.partial(gather_kernel, planes),
        out_shape=(
            jax.ShapeDtypeStruct((span, heads * D), q.dtype),
            jax.ShapeDtypeStruct((span, heads * D), g.dtype),
            jax.ShapeDtypeStruct((window, D), k.dtype),
            jax.ShapeDtypeStruct((window, D), v.dtype),
            jax.ShapeDtypeStruct((heads, span), lse.dtype),
            jax.ShapeDtypeStruct((heads, span), delta.dtype),
            jax.ShapeDtypeStruct((seg.shape[0], window), seg.dtype),
        ),
        in_specs=[any_space] * 7,
        out_specs=(any_space,) * 7,
        scratch_shapes=[
            pltpu.SemaphoreType.DMA((7, PLANE - 1)),
            pltpu.SemaphoreType.DMA((7, PLANE - 1)),
            pltpu.SemaphoreType.DMA((3, HALO)),
            pltpu.SemaphoreType.DMA((3, HALO)),
            pltpu.SemaphoreType.DMA((7,)),
        ],
        compiler_params=pltpu.CompilerParams(collective_id=0, has_side_effects=True),
        name="gather_plane",
    )(q, g, k, v, lse, delta, seg)


def attend_kernel(
    bounds, start, lse, delta, q, g, k, v, dq, dk_halo, dv_halo, dk_own, dv_own, dk, dv, k_t
):
    head = pl.program_id(0)
    span = q.shape[0]
    own = k.shape[0] - span
    inv_root = 1.0 / math.sqrt(D)
    scale = inv_root * LOG2E

    @pl.when(head == 0)
    def _():
        dk[...] = jnp.zeros_like(dk)
        dv[...] = jnp.zeros_like(dv)
        k_t[...] = k[...].T

    @pl.loop(0, span // BLOCK)
    def _(i):
        here = pl.ds(pl.multiple_of(i * BLOCK, BLOCK), BLOCK)
        q_rows, g_rows = q[here, :], g[here, :]
        lse_row = lse[0, :, here] * LOG2E
        delta_row = delta[0, :, here]
        start_row = start[:, here]

        def tile(masked, j, dq_t):
            there = pl.ds(pl.multiple_of(j * BLOCK, BLOCK), BLOCK)
            k_rows, v_rows = k[there, :], v[there, :]
            nt = (((1,), (1,)), ((), ()))
            scores = lax.dot_general(k_rows, q_rows, nt, preferred_element_type=jnp.float32)
            weights = jnp.exp2(scores * scale - lse_row)
            if masked:
                key_at = j * BLOCK + lax.broadcasted_iota(jnp.int32, (BLOCK, BLOCK), 0)
                query_at = own + i * BLOCK + lax.broadcasted_iota(jnp.int32, (BLOCK, BLOCK), 1)
                weights = jnp.where((key_at >= start_row) & (key_at <= query_at), weights, 0.0)
            d_weights = lax.dot_general(v_rows, g_rows, nt, preferred_element_type=jnp.float32)
            dscore = (weights * (d_weights - delta_row)).astype(jnp.bfloat16)
            low = weights.astype(jnp.bfloat16)
            dv[there, :] += jnp.dot(low, g_rows, preferred_element_type=jnp.float32)
            dk[there, :] += jnp.dot(dscore, q_rows, preferred_element_type=jnp.float32)
            return dq_t + jnp.dot(k_t[:, there], dscore, preferred_element_type=jnp.float32)

        diagonal = own // BLOCK + i
        low_end, full = bounds[0, i], bounds[1, i]
        dq_t = jnp.zeros((D, BLOCK), jnp.float32)
        dq_t = lax.fori_loop(low_end, full, functools.partial(tile, True), dq_t)
        dq_t = lax.fori_loop(full, diagonal, functools.partial(tile, False), dq_t)
        dq_t = tile(True, diagonal, dq_t)
        dq[here, :] = (dq_t.T * inv_root).astype(dq.dtype)

    @pl.when(head == pl.num_programs(0) - 1)
    def _():
        dk_halo[...] = (dk[:own, :] * inv_root).astype(dk_halo.dtype)
        dv_halo[...] = dv[:own, :].astype(dv_halo.dtype)
        dk_own[...] = dk[own:, :] * inv_root
        dv_own[...] = dv[own:, :]


def attend(q, g, k, v, lse, delta, seg_win, planes):
    span = q.shape[0]
    heads = q.shape[1] // D
    window = k.shape[0]
    own = window - span
    plane = lax.axis_index("seq") // PLANE
    at = jnp.arange(window, dtype=jnp.int32)
    ids = jnp.where(at >= own - plane * span, seg_win[0], -1)
    own_ids = ids[own:]
    start = jnp.sum((ids[None, :] < own_ids[:, None]).astype(jnp.int32), axis=1)
    tiles = span // BLOCK
    edge = start.reshape(tiles, BLOCK)
    diagonal = own // BLOCK + jnp.arange(tiles, dtype=jnp.int32)
    low_end = edge[:, 0] // BLOCK
    full = jnp.minimum((edge[:, -1] + BLOCK - 1) // BLOCK, diagonal)
    bounds = jnp.stack([low_end, jnp.maximum(full, low_end)])
    column = pl.BlockSpec((span, D), lambda h, b: (0, h))
    row = pl.BlockSpec((1, 1, span), lambda h, b: (h, 0, 0))

    def whole(shape):
        return pl.BlockSpec(shape, lambda h, b: (0, 0))

    return pl.pallas_call(
        attend_kernel,
        grid_spec=pltpu.PrefetchScalarGridSpec(
            num_scalar_prefetch=1,
            grid=(heads,),
            in_specs=[whole((1, span)), row, row, column, column, whole((window, D)), whole((window, D))],
            out_specs=[column, whole((own, D)), whole((own, D)), whole((span, D)), whole((span, D))],
            scratch_shapes=[
                pltpu.VMEM((window, D), jnp.float32),
                pltpu.VMEM((window, D), jnp.float32),
                pltpu.VMEM((D, window), jnp.bfloat16),
            ],
        ),
        out_shape=(
            jax.ShapeDtypeStruct((span, heads * D), q.dtype),
            jax.ShapeDtypeStruct((own, D), jnp.bfloat16),
            jax.ShapeDtypeStruct((own, D), jnp.bfloat16),
            jax.ShapeDtypeStruct((span, D), jnp.float32),
            jax.ShapeDtypeStruct((span, D), jnp.float32),
        ),
        compiler_params=pltpu.CompilerParams(vmem_limit_bytes=48 * 1024 * 1024),
        name="attend",
    )(bounds, start[None, :], lse[:, None, :], delta[:, None, :], q, g, k, v)


def scatter_kernel(
    planes, dq, dk_halo, dv_halo, dk_own, dv_own, grad_q, grad_k, grad_v,
    dk_in, dv_in, dk_low, dv_low, total, send, recv, z_send, z_recv, last_send, last_recv, local,
):
    rows = grad_q.shape[0]
    span = rows * PLANE
    wide = dq.shape[1]
    me = lax.axis_index("seq")
    plane, rank = me // PLANE, lax.rem(me, PLANE)

    def cols(index, width):
        return pl.ds(pl.multiple_of(index * width, width), width)

    def z_copy(n, dz):
        halo, into = ((dk_halo, dk_in), (dv_halo, dv_in))[n]
        return pltpu.make_async_remote_copy(
            halo.at[pl.ds((HALO - dz) * span, span), :], into.at[dz - 1],
            z_send.at[n, dz - 1], z_recv.at[n, dz - 1],
            device_id=dev(me - dz * PLANE), device_id_type=MESH,
        )

    def q_copy(o, origin):
        peer = lax.rem(rank + o, PLANE)
        return pltpu.make_async_remote_copy(
            dq.at[cols(peer, rows), :], grad_q.at[:, cols(origin, wide)], send.at[o - 1], recv.at[o - 1],
            device_id=dev(plane * PLANE + peer), device_id_type=MESH,
        )

    def kv_copy(n, o, origin):
        low, out = ((dk_low, grad_k), (dv_low, grad_v))[n]
        peer = lax.rem(rank + o, PLANE)
        return pltpu.make_async_remote_copy(
            low.at[cols(peer, rows), :], out.at[:, cols(origin, D)], last_send.at[n, o - 1], last_recv.at[n, o - 1],
            device_id=dev(plane * PLANE + peer), device_id_type=MESH,
        )

    greet(me, plane, rank, planes)
    for n in range(2):
        for dz in range(1, HALO + 1):
            @pl.when(plane >= dz)
            def _():
                z_copy(n, dz).start()
    for o in range(1, PLANE):
        q_copy(o, rank).start()
    own_q = pltpu.make_async_copy(dq.at[cols(rank, rows), :], grad_q.at[:, cols(rank, wide)], local.at[0])
    own_q.start()
    own_kv = []
    for n in range(2):
        low, out, own, into = ((dk_low, grad_k, dk_own, dk_in), (dv_low, grad_v, dv_own, dv_in))[n]
        total[...] = own[...]
        for dz in range(1, HALO + 1):
            @pl.when(plane + dz < planes)
            def _():
                z_copy(n, dz).wait_recv()
                total[...] += into[dz - 1].astype(jnp.float32)
        low[...] = total[...].astype(low.dtype)
        for o in range(1, PLANE):
            kv_copy(n, o, rank).start()
        own_kv.append(pltpu.make_async_copy(low.at[cols(rank, rows), :], out.at[:, cols(rank, D)], local.at[1 + n]))
        own_kv[n].start()
    own_q.wait()
    for n in range(2):
        own_kv[n].wait()
        for dz in range(1, HALO + 1):
            @pl.when(plane >= dz)
            def _():
                z_copy(n, dz).wait_send()
    for o in range(1, PLANE):
        origin = lax.rem(rank + PLANE - o, PLANE)
        q_copy(o, origin).wait()
        for n in range(2):
            kv_copy(n, o, origin).wait()


def scatter(dq, dk_halo, dv_halo, dk_own, dv_own, planes):
    span, wide = dq.shape
    rows = span // PLANE
    any_space = pl.BlockSpec(memory_space=pl.ANY)
    vmem = pl.BlockSpec(memory_space=pltpu.VMEM)
    return pl.pallas_call(
        functools.partial(scatter_kernel, planes),
        out_shape=(
            jax.ShapeDtypeStruct((rows, PLANE * wide), dq.dtype),
            jax.ShapeDtypeStruct((rows, PLANE * D), jnp.bfloat16),
            jax.ShapeDtypeStruct((rows, PLANE * D), jnp.bfloat16),
        ),
        in_specs=[any_space] * 3 + [vmem] * 2,
        out_specs=(any_space,) * 3,
        scratch_shapes=[
            pltpu.VMEM((HALO, span, D), jnp.bfloat16),
            pltpu.VMEM((HALO, span, D), jnp.bfloat16),
            pltpu.VMEM((span, D), jnp.bfloat16),
            pltpu.VMEM((span, D), jnp.bfloat16),
            pltpu.VMEM((span, D), jnp.float32),
            pltpu.SemaphoreType.DMA((PLANE - 1,)),
            pltpu.SemaphoreType.DMA((PLANE - 1,)),
            pltpu.SemaphoreType.DMA((2, HALO)),
            pltpu.SemaphoreType.DMA((2, HALO)),
            pltpu.SemaphoreType.DMA((2, PLANE - 1)),
            pltpu.SemaphoreType.DMA((2, PLANE - 1)),
            pltpu.SemaphoreType.DMA((3,)),
        ],
        compiler_params=pltpu.CompilerParams(
            collective_id=1, has_side_effects=True, vmem_limit_bytes=32 * 1024 * 1024
        ),
        name="scatter_plane",
    )(dq, dk_halo, dv_halo, dk_own, dv_own)


def on_device(queries, keys, values, outputs, out_grad, lse, segments):
    rows = queries.shape[0]
    heads = lse.shape[0]
    planes = lax.axis_size("seq") // PLANE
    delta = jnp.sum(
        (outputs.astype(jnp.float32) * out_grad.astype(jnp.float32)).reshape(rows, heads, D), axis=2
    ).T
    seg = jnp.broadcast_to(segments[None, :], (8, rows))
    q, g, k, v, lse_all, delta_all, seg_win = gather(
        queries, out_grad, keys, values, lse, delta, seg, planes
    )
    dq, dk_halo, dv_halo, dk_own, dv_own = attend(q, g, k, v, lse_all, delta_all, seg_win, planes)
    return scatter(dq, dk_halo, dv_halo, dk_own, dv_own, planes)


def solution(mesh):
    rows = P(("dp", "seq"), None)
    in_specs = (rows, rows, rows, rows, rows, P(None, ("dp", "seq")), P(("dp", "seq")))
    return jax.shard_map(
        on_device, mesh=mesh, in_specs=in_specs, out_specs=(rows, rows, rows), check_vma=False
    )
```

```python
import functools
import math

import jax
import jax.numpy as jnp
from jax import lax
from jax.experimental import pallas as pl
from jax.experimental.pallas import tpu as pltpu
from jax.sharding import PartitionSpec as P

D = 128
LOG2E = math.log2(math.e)
MESH = pl.DeviceIdType.MESH
PLANE = 8
HALO = 2
BLOCK = 256
VMEM_LIMIT = 60 * 1024 * 1024


def dev(index):
    return {"seq": index}


def greet(me, plane, rank, planes):
    barrier = pltpu.get_barrier_semaphore()
    for o in range(1, PLANE):
        peer = plane * PLANE + lax.rem(rank + o, PLANE)
        pl.semaphore_signal(barrier, inc=1, device_id=dev(peer), device_id_type=MESH)
    count = PLANE - 1
    for dz in range(1, HALO + 1):
        up = plane + dz < planes
        down = plane >= dz

        @pl.when(up)
        def _():
            pl.semaphore_signal(barrier, inc=1, device_id=dev(me + dz * PLANE), device_id_type=MESH)

        @pl.when(down)
        def _():
            pl.semaphore_signal(barrier, inc=1, device_id=dev(me - dz * PLANE), device_id_type=MESH)

        count = count + up.astype(jnp.int32) + down.astype(jnp.int32)
    pl.semaphore_wait(barrier, count)


def gather_kernel(
    planes, q, g, o, k, v, seg, lse, q_all, g_all, k_win, v_win, stats_all, seg_win,
    o_here, g_here, stats, seg_here, send, recv, z_send, z_recv, local,
):
    rows = q.shape[0]
    span = rows * PLANE
    wide = q_all.shape[1]
    heads = wide // D
    me = lax.axis_index("seq")
    plane, rank = me // PLANE, lax.rem(me, PLANE)
    own = HALO * span

    def part(index, width):
        return pl.ds(pl.multiple_of(index * width, width), width)

    def own_part(s):
        return pl.ds(pl.multiple_of(own + s * rows, rows), rows)

    pieces = [
        (lambda p: seg_here, lambda s: seg_win.at[:, own_part(s)]),
        (lambda p: k.at[:, part(p, D)], lambda s: k_win.at[own_part(s), :]),
        (lambda p: v.at[:, part(p, D)], lambda s: v_win.at[own_part(s), :]),
        (lambda p: q.at[:, part(p, wide)], lambda s: q_all.at[part(s, rows), :]),
        (lambda p: g.at[:, part(p, wide)], lambda s: g_all.at[part(s, rows), :]),
        (lambda p: stats.at[part(p, 2 * heads), :], lambda s: stats_all.at[:, part(s, rows)]),
    ]
    last = len(pieces) - 1

    def own_copy(n):
        source, target = pieces[n]
        return pltpu.make_async_copy(source(rank), target(rank), local.at[n])

    def plane_copy(n, o):
        source, target = pieces[n]
        peer = lax.rem(rank + o, PLANE)
        return pltpu.make_async_remote_copy(
            source(peer), target(rank), send.at[n, o - 1], recv.at[n, o - 1],
            device_id=dev(plane * PLANE + peer), device_id_type=MESH,
        )

    def arrival(n, o):
        source, target = pieces[n]
        origin = lax.rem(rank + PLANE - o, PLANE)
        return pltpu.make_async_remote_copy(
            source(rank), target(origin), send.at[n, o - 1], recv.at[n, o - 1],
            device_id=dev(plane * PLANE + origin), device_id_type=MESH,
        )

    def z_copy(n, dz):
        if n == 0:
            whole = seg_win.at[:, pl.ds(own, span)]
            there = seg_win.at[:, pl.ds(own - dz * span, span)]
        else:
            win = (k_win, v_win)[n - 1]
            whole = win.at[pl.ds(own, span), :]
            there = win.at[pl.ds(own - dz * span, span), :]
        return pltpu.make_async_remote_copy(
            whole, there, z_send.at[n, dz - 1], z_recv.at[n, dz - 1],
            device_id=dev(me + dz * PLANE), device_id_type=MESH,
        )

    load_o = pltpu.make_async_copy(o, o_here, local.at[last + 1])
    load_g = pltpu.make_async_copy(g, g_here, local.at[last + 2])
    load_o.start()
    load_g.start()
    seg_here[...] = jnp.broadcast_to(seg[...], seg_here.shape)
    greet(me, plane, rank, planes)
    for n in range(last):
        for o_at in range(1, PLANE):
            plane_copy(n, o_at).start()
        own_copy(n).start()

    load_o.wait()
    load_g.wait()

    @pl.loop(0, PLANE)
    def _(p):
        sums = []
        for h in range(heads):
            features = pl.ds(pl.multiple_of(p * wide + h * D, D), D)
            product = o_here[:, features].astype(jnp.float32) * g_here[:, features].astype(jnp.float32)
            sums.append(jnp.sum(product.T, axis=0, keepdims=True))
        stats[pl.ds(pl.multiple_of(p * 2 * heads, heads), heads), :] = lse[pl.ds(pl.multiple_of(p * heads, heads), heads), :]
        stats[pl.ds(pl.multiple_of((p * 2 + 1) * heads, heads), heads), :] = jnp.concatenate(sums, axis=0)

    for o_at in range(1, PLANE):
        plane_copy(last, o_at).start()
    own_copy(last).start()

    for n in range(3):
        own_copy(n).wait()
        for o_at in range(1, PLANE):
            arrival(n, o_at).wait_recv()
        for dz in range(1, HALO + 1):
            @pl.when(plane + dz < planes)
            def _():
                z_copy(n, dz).start()
    for n in range(3, last + 1):
        own_copy(n).wait()
        for o_at in range(1, PLANE):
            arrival(n, o_at).wait_recv()
    for n in range(last + 1):
        for o_at in range(1, PLANE):
            plane_copy(n, o_at).wait_send()
    for n in range(3):
        for dz in range(1, HALO + 1):
            @pl.when(plane + dz < planes)
            def _():
                z_copy(n, dz).wait_send()

            @pl.when(plane >= dz)
            def _():
                z_copy(n, dz).wait_recv()


def gather(q, g, o, k, v, seg, lse, planes):
    rows = q.shape[0]
    span = rows * PLANE
    heads = lse.shape[0] // PLANE
    window = (HALO + 1) * span
    any_space = pl.BlockSpec(memory_space=pl.ANY)
    vmem = pl.BlockSpec(memory_space=pltpu.VMEM)
    return pl.pallas_call(
        functools.partial(gather_kernel, planes),
        out_shape=(
            jax.ShapeDtypeStruct((span, heads * D), q.dtype),
            jax.ShapeDtypeStruct((span, heads * D), g.dtype),
            jax.ShapeDtypeStruct((window, D), k.dtype),
            jax.ShapeDtypeStruct((window, D), v.dtype),
            jax.ShapeDtypeStruct((2 * heads, span), lse.dtype),
            jax.ShapeDtypeStruct((8, window), seg.dtype),
        ),
        in_specs=[any_space] * 5 + [vmem] * 2,
        out_specs=(any_space,) * 6,
        scratch_shapes=[
            pltpu.VMEM(o.shape, o.dtype),
            pltpu.VMEM(g.shape, g.dtype),
            pltpu.VMEM((2 * heads * PLANE, rows), jnp.float32),
            pltpu.VMEM((8, rows), jnp.int32),
            pltpu.SemaphoreType.DMA((6, PLANE - 1)),
            pltpu.SemaphoreType.DMA((6, PLANE - 1)),
            pltpu.SemaphoreType.DMA((3, HALO)),
            pltpu.SemaphoreType.DMA((3, HALO)),
            pltpu.SemaphoreType.DMA((8,)),
        ],
        compiler_params=pltpu.CompilerParams(
            collective_id=0, has_side_effects=True, vmem_limit_bytes=VMEM_LIMIT
        ),
        name="gather_plane",
    )(q, g, o, k, v, seg, lse)


def attend_kernel(
    seg, stats, q, g, k, v, dq, dk_halo, dv_halo, dk_own, dv_own, dk, dv, k_t, start
):
    i = pl.program_id(0)
    window = k.shape[0]
    span = dk_own.shape[0]
    own = window - span
    heads = q.shape[1] // D
    across = heads * BLOCK
    inv_root = 1.0 / math.sqrt(D)
    scale = inv_root * LOG2E

    @pl.when(i == 0)
    def _():
        dk[...] = jnp.zeros_like(dk)
        dv[...] = jnp.zeros_like(dv)
        k_t[...] = k[...].T
        ids = seg[...]
        at = lax.broadcasted_iota(jnp.int32, ids.shape, 1)
        plane = lax.axis_index("seq") // PLANE
        first = own - jnp.minimum(plane, HALO) * span
        begins = (ids != pltpu.roll(ids, 1, 1)) & (at > first)
        found = jnp.where(begins, at, first)
        step = 1
        while step < window:
            found = jnp.where(at >= step, jnp.maximum(found, pltpu.roll(found, step, 1)), found)
            step *= 2
        start[...] = found[:, own:]

    def stacked(ref):
        return jnp.concatenate([ref[:, h * D:(h + 1) * D] for h in range(heads)], axis=0)

    def in_line(first):
        return jnp.concatenate([stats[first + h:first + h + 1, :] for h in range(heads)], axis=1)

    q_rows, g_rows = stacked(q), stacked(g)
    lse_row = in_line(0) * LOG2E
    delta_row = in_line(heads)
    block_start = start[0:1, pl.ds(pl.multiple_of(i * BLOCK, BLOCK), BLOCK)]
    start_row = jnp.concatenate([block_start] * heads, axis=1)
    query_row = own + i * BLOCK + lax.rem(lax.broadcasted_iota(jnp.int32, (1, across), 1), BLOCK)

    def tile(masked, j, dq_t):
        there = pl.ds(pl.multiple_of(j * BLOCK, BLOCK), BLOCK)
        k_rows, v_rows = k[there, :], v[there, :]
        nt = (((1,), (1,)), ((), ()))
        scores = lax.dot_general(k_rows, q_rows, nt, preferred_element_type=jnp.float32)
        weights = jnp.exp2(scores * scale - lse_row)
        if masked:
            key_at = j * BLOCK + lax.broadcasted_iota(jnp.int32, (BLOCK, across), 0)
            weights = jnp.where((key_at >= start_row) & (key_at <= query_row), weights, 0.0)
        d_weights = lax.dot_general(v_rows, g_rows, nt, preferred_element_type=jnp.float32)
        dscore = (weights * (d_weights - delta_row)).astype(jnp.bfloat16)
        low = weights.astype(jnp.bfloat16)
        dv[there, :] += jnp.dot(low, g_rows, preferred_element_type=jnp.float32)
        dk[there, :] += jnp.dot(dscore, q_rows, preferred_element_type=jnp.float32)
        return dq_t + jnp.dot(k_t[:, there], dscore, preferred_element_type=jnp.float32)

    position = block_start.astype(jnp.float32)
    diagonal = own // BLOCK + i
    low_end = jnp.min(position).astype(jnp.int32) // BLOCK
    full = (jnp.max(position).astype(jnp.int32) + BLOCK - 1) // BLOCK
    full = jnp.clip(full, low_end, diagonal)
    dq_t = jnp.zeros((D, across), jnp.float32)
    dq_t = lax.fori_loop(low_end, full, functools.partial(tile, True), dq_t)
    dq_t = lax.fori_loop(full, diagonal, functools.partial(tile, False), dq_t)
    dq_t = tile(True, diagonal, dq_t)
    for h in range(heads):
        dq[:, h * D:(h + 1) * D] = (dq_t[:, h * BLOCK:(h + 1) * BLOCK].T * inv_root).astype(dq.dtype)

    @pl.when(i == pl.num_programs(0) - 1)
    def _():
        dk_halo[...] = (dk[:own, :] * inv_root).astype(dk_halo.dtype)
        dv_halo[...] = dv[:own, :].astype(dv_halo.dtype)
        dk_own[...] = dk[own:, :] * inv_root
        dv_own[...] = dv[own:, :]


def attend(q, g, k, v, stats, seg_win):
    span, wide = q.shape
    window = k.shape[0]
    own = window - span
    block = pl.BlockSpec((BLOCK, wide), lambda i: (i, 0))

    def whole(shape):
        return pl.BlockSpec(shape, lambda i: (0, 0))

    return pl.pallas_call(
        attend_kernel,
        grid=(span // BLOCK,),
        in_specs=[
            whole(seg_win.shape), pl.BlockSpec((stats.shape[0], BLOCK), lambda i: (0, i)),
            block, block, whole((window, D)), whole((window, D)),
        ],
        out_specs=[block, whole((own, D)), whole((own, D)), whole((span, D)), whole((span, D))],
        out_shape=(
            jax.ShapeDtypeStruct((span, wide), q.dtype),
            jax.ShapeDtypeStruct((own, D), jnp.bfloat16),
            jax.ShapeDtypeStruct((own, D), jnp.bfloat16),
            jax.ShapeDtypeStruct((span, D), jnp.float32),
            jax.ShapeDtypeStruct((span, D), jnp.float32),
        ),
        scratch_shapes=[
            pltpu.VMEM((window, D), jnp.float32),
            pltpu.VMEM((window, D), jnp.float32),
            pltpu.VMEM((D, window), jnp.bfloat16),
            pltpu.VMEM((8, span), jnp.int32),
        ],
        compiler_params=pltpu.CompilerParams(vmem_limit_bytes=VMEM_LIMIT),
        name="attend",
    )(seg_win, stats, q, g, k, v)


def scatter_kernel(
    planes, dq, dk_halo, dv_halo, dk_own, dv_own, grad_q, grad_k, grad_v,
    dk_in, dv_in, dk_low, dv_low, total, send, recv, z_send, z_recv, last_send, last_recv, local,
):
    rows = grad_q.shape[0]
    span = rows * PLANE
    wide = dq.shape[1]
    me = lax.axis_index("seq")
    plane, rank = me // PLANE, lax.rem(me, PLANE)

    def cols(index, width):
        return pl.ds(pl.multiple_of(index * width, width), width)

    def z_copy(n, dz):
        halo, into = ((dk_halo, dk_in), (dv_halo, dv_in))[n]
        return pltpu.make_async_remote_copy(
            halo.at[pl.ds((HALO - dz) * span, span), :], into.at[dz - 1],
            z_send.at[n, dz - 1], z_recv.at[n, dz - 1],
            device_id=dev(me - dz * PLANE), device_id_type=MESH,
        )

    def q_copy(o, origin):
        peer = lax.rem(rank + o, PLANE)
        return pltpu.make_async_remote_copy(
            dq.at[cols(peer, rows), :], grad_q.at[:, cols(origin, wide)], send.at[o - 1], recv.at[o - 1],
            device_id=dev(plane * PLANE + peer), device_id_type=MESH,
        )

    def kv_copy(n, o, origin):
        low, out = ((dk_low, grad_k), (dv_low, grad_v))[n]
        peer = lax.rem(rank + o, PLANE)
        return pltpu.make_async_remote_copy(
            low.at[cols(peer, rows), :], out.at[:, cols(origin, D)], last_send.at[n, o - 1], last_recv.at[n, o - 1],
            device_id=dev(plane * PLANE + peer), device_id_type=MESH,
        )

    greet(me, plane, rank, planes)
    for n in range(2):
        for dz in range(1, HALO + 1):
            @pl.when(plane >= dz)
            def _():
                z_copy(n, dz).start()
    for o in range(1, PLANE):
        q_copy(o, rank).start()
    own_q = pltpu.make_async_copy(dq.at[cols(rank, rows), :], grad_q.at[:, cols(rank, wide)], local.at[0])
    own_q.start()
    own_kv = []
    for n in range(2):
        low, out, own, into = ((dk_low, grad_k, dk_own, dk_in), (dv_low, grad_v, dv_own, dv_in))[n]
        total[...] = own[...]
        for dz in range(1, HALO + 1):
            @pl.when(plane + dz < planes)
            def _():
                z_copy(n, dz).wait_recv()
                total[...] += into[dz - 1].astype(jnp.float32)
        low[...] = total[...].astype(low.dtype)
        for o in range(1, PLANE):
            kv_copy(n, o, rank).start()
        own_kv.append(pltpu.make_async_copy(low.at[cols(rank, rows), :], out.at[:, cols(rank, D)], local.at[1 + n]))
        own_kv[n].start()
    own_q.wait()
    for n in range(2):
        own_kv[n].wait()
        for dz in range(1, HALO + 1):
            @pl.when(plane >= dz)
            def _():
                z_copy(n, dz).wait_send()
    for o in range(1, PLANE):
        origin = lax.rem(rank + PLANE - o, PLANE)
        q_copy(o, origin).wait()
        for n in range(2):
            kv_copy(n, o, origin).wait()


def scatter(dq, dk_halo, dv_halo, dk_own, dv_own, planes):
    span, wide = dq.shape
    rows = span // PLANE
    any_space = pl.BlockSpec(memory_space=pl.ANY)
    vmem = pl.BlockSpec(memory_space=pltpu.VMEM)
    return pl.pallas_call(
        functools.partial(scatter_kernel, planes),
        out_shape=(
            jax.ShapeDtypeStruct((rows, PLANE * wide), dq.dtype),
            jax.ShapeDtypeStruct((rows, PLANE * D), jnp.bfloat16),
            jax.ShapeDtypeStruct((rows, PLANE * D), jnp.bfloat16),
        ),
        in_specs=[any_space] * 3 + [vmem] * 2,
        out_specs=(any_space,) * 3,
        scratch_shapes=[
            pltpu.VMEM((HALO, span, D), jnp.bfloat16),
            pltpu.VMEM((HALO, span, D), jnp.bfloat16),
            pltpu.VMEM((span, D), jnp.bfloat16),
            pltpu.VMEM((span, D), jnp.bfloat16),
            pltpu.VMEM((span, D), jnp.float32),
            pltpu.SemaphoreType.DMA((PLANE - 1,)),
            pltpu.SemaphoreType.DMA((PLANE - 1,)),
            pltpu.SemaphoreType.DMA((2, HALO)),
            pltpu.SemaphoreType.DMA((2, HALO)),
            pltpu.SemaphoreType.DMA((2, PLANE - 1)),
            pltpu.SemaphoreType.DMA((2, PLANE - 1)),
            pltpu.SemaphoreType.DMA((3,)),
        ],
        compiler_params=pltpu.CompilerParams(
            collective_id=1, has_side_effects=True, vmem_limit_bytes=VMEM_LIMIT
        ),
        name="scatter_plane",
    )(dq, dk_halo, dv_halo, dk_own, dv_own)


def on_device(queries, keys, values, outputs, out_grad, lse, segments):
    planes = lax.axis_size("seq") // PLANE
    q, g, k, v, stats, seg_win = gather(
        queries, out_grad, outputs, keys, values, segments[None, :], lse, planes
    )
    return scatter(*attend(q, g, k, v, stats, seg_win), planes)


def solution(mesh):
    rows = P(("dp", "seq"), None)
    in_specs = (rows, rows, rows, rows, rows, P(None, ("dp", "seq")), P(("dp", "seq")))
    return jax.shard_map(
        on_device, mesh=mesh, in_specs=in_specs, out_specs=(rows, rows, rows), check_vma=False
    )
```

```python
import functools
import math

import jax
import jax.numpy as jnp
from jax import lax
from jax.experimental import pallas as pl
from jax.experimental.pallas import tpu as pltpu
from jax.sharding import PartitionSpec as P

D = 128
LOG2E = math.log2(math.e)
MESH = pl.DeviceIdType.MESH
PLANE = 8
PLANE_X = 4
HALO = 2
CHUNKS = 2
ROUTE_SEMS = 10
BLOCK = 256
VMEM_LIMIT = 60 * 1024 * 1024


def dev(index):
    return {"seq": index}


def greet(me, plane, rank, planes):
    barrier = pltpu.get_barrier_semaphore()
    for o in range(1, PLANE):
        peer = plane * PLANE + lax.rem(rank + o, PLANE)
        pl.semaphore_signal(barrier, inc=1, device_id=dev(peer), device_id_type=MESH)
    count = PLANE - 1
    for dz in range(1, HALO + 1):
        up = plane + dz < planes
        down = plane >= dz

        @pl.when(up)
        def _():
            pl.semaphore_signal(barrier, inc=1, device_id=dev(me + dz * PLANE), device_id_type=MESH)

        @pl.when(down)
        def _():
            pl.semaphore_signal(barrier, inc=1, device_id=dev(me - dz * PLANE), device_id_type=MESH)

        count = count + up.astype(jnp.int32) + down.astype(jnp.int32)
    pl.semaphore_wait(barrier, count)


class Route:
    def __init__(self, x_first, plane, rank, source, target, stage, sems):
        self.x_first, self.plane = x_first, plane
        self.y, self.x = rank // PLANE_X, lax.rem(rank, PLANE_X)
        self.source, self.target, self.stage = source, target, stage
        self.send, self.recv = sems

    def rank(self, dy, dx):
        y = self.y if dy == 0 else 1 - self.y
        return y * PLANE_X + lax.rem(self.x + dx + PLANE_X, PLANE_X)

    def copy(self, n, source, target, peer):
        return pltpu.make_async_remote_copy(
            source, target, self.send.at[n], self.recv.at[n],
            device_id=dev(self.plane * PLANE + peer), device_id_type=MESH,
        )

    def first_leg(self, dx):
        peer = self.rank(0, dx) if self.x_first else self.rank(1, 0)
        return self.copy(dx - 1, self.source(self.rank(1, dx)), self.stage.at[dx - 1], peer)

    def second_leg(self, dx):
        if self.x_first:
            origin, peer = self.rank(0, -dx), self.rank(1, 0)
        else:
            origin, peer = self.rank(1, 0), self.rank(0, dx)
        return self.copy(2 + dx, self.stage.at[dx - 1], self.target(origin), peer)

    def straight(self, dx):
        peer = self.rank(0, dx) if dx else self.rank(1, 0)
        return self.copy(6 + dx, self.source(peer), self.target(self.rank(0, 0)), peer)

    def start_first(self):
        for dx in range(1, PLANE_X):
            self.first_leg(dx).start()

    def start_straight(self):
        for dx in range(PLANE_X):
            self.straight(dx).start()

    def pass_on(self):
        for dx in range(1, PLANE_X):
            self.first_leg(dx).wait_recv()
            self.second_leg(dx).start()

    def wait_arrivals(self):
        for dx in range(PLANE_X):
            origin = self.rank(0, -dx) if dx else self.rank(1, 0)
            self.copy(6 + dx, self.target(origin), self.target(origin), origin).wait_recv()
        for dx in range(1, PLANE_X):
            origin = self.rank(1, -dx)
            self.copy(2 + dx, self.target(origin), self.target(origin), origin).wait_recv()

    def wait_sends(self):
        for dx in range(1, PLANE_X):
            self.first_leg(dx).wait_send()
            self.second_leg(dx).wait_send()
        for dx in range(PLANE_X):
            self.straight(dx).wait_send()


def gather_kernel(
    planes, q, g, o, k, v, seg, lse, q_all, g_all, k_win, v_win, stats_all, seg_win,
    o_here, g_here, stats, seg_here, stage, r_send, r_recv, send, recv, z_send, z_recv, local,
):
    rows = q.shape[0]
    span = rows * PLANE
    wide = q_all.shape[1]
    heads = wide // D
    me = lax.axis_index("seq")
    plane, rank = me // PLANE, lax.rem(me, PLANE)
    own = HALO * span

    def part(index, width):
        return pl.ds(pl.multiple_of(index * width, width), width)

    def own_part(s):
        return pl.ds(pl.multiple_of(own + s * rows, rows), rows)

    pieces = [
        (lambda p: seg_here, lambda s: seg_win.at[:, own_part(s)]),
        (lambda p: k.at[:, part(p, D)], lambda s: k_win.at[own_part(s), :]),
        (lambda p: v.at[:, part(p, D)], lambda s: v_win.at[own_part(s), :]),
        (lambda p: stats.at[part(p, 2 * heads), :], lambda s: stats_all.at[:, part(s, rows)]),
        (lambda p: q.at[:, part(p, wide)], lambda s: q_all.at[part(s, rows), :]),
        (lambda p: g.at[:, part(p, wide)], lambda s: g_all.at[part(s, rows), :]),
    ]
    last = 3
    narrow = wide // CHUNKS

    def route(n, c):
        array, gathered = ((q, q_all), (g, g_all))[n]

        def source(p):
            return array.at[:, pl.ds(pl.multiple_of(p * wide + c * narrow, narrow), narrow)]

        def target(s):
            return gathered.at[part(s, rows), pl.ds(c * narrow, narrow)]

        return Route(
            n == 0, plane, rank, source, target, stage.at[n, c], (r_send.at[n, c], r_recv.at[n, c])
        )

    routes = [route(n, c) for c in range(CHUNKS) for n in range(2)]

    def own_copy(n):
        source, target = pieces[n]
        return pltpu.make_async_copy(source(rank), target(rank), local.at[n])

    def plane_copy(n, o):
        source, target = pieces[n]
        peer = lax.rem(rank + o, PLANE)
        return pltpu.make_async_remote_copy(
            source(peer), target(rank), send.at[n, o - 1], recv.at[n, o - 1],
            device_id=dev(plane * PLANE + peer), device_id_type=MESH,
        )

    def arrival(n, o):
        source, target = pieces[n]
        origin = lax.rem(rank + PLANE - o, PLANE)
        return pltpu.make_async_remote_copy(
            source(rank), target(origin), send.at[n, o - 1], recv.at[n, o - 1],
            device_id=dev(plane * PLANE + origin), device_id_type=MESH,
        )

    def z_copy(n, dz):
        if n == 0:
            whole = seg_win.at[:, pl.ds(own, span)]
            there = seg_win.at[:, pl.ds(own - dz * span, span)]
        else:
            win = (k_win, v_win)[n - 1]
            whole = win.at[pl.ds(own, span), :]
            there = win.at[pl.ds(own - dz * span, span), :]
        return pltpu.make_async_remote_copy(
            whole, there, z_send.at[n, dz - 1], z_recv.at[n, dz - 1],
            device_id=dev(me + dz * PLANE), device_id_type=MESH,
        )

    load_o = pltpu.make_async_copy(o, o_here, local.at[6])
    load_g = pltpu.make_async_copy(g, g_here, local.at[7])
    load_o.start()
    load_g.start()
    seg_here[...] = jnp.broadcast_to(seg[...], seg_here.shape)
    greet(me, plane, rank, planes)
    for n in range(last):
        for o_at in range(1, PLANE):
            plane_copy(n, o_at).start()
        own_copy(n).start()
    for path in routes:
        path.start_first()
    for path in routes:
        path.start_straight()
    own_copy(4).start()
    own_copy(5).start()

    load_o.wait()
    load_g.wait()

    @pl.loop(0, PLANE)
    def _(p):
        sums = []
        for h in range(heads):
            features = pl.ds(pl.multiple_of(p * wide + h * D, D), D)
            product = o_here[:, features].astype(jnp.float32) * g_here[:, features].astype(jnp.float32)
            sums.append(jnp.sum(product.T, axis=0, keepdims=True))
        stats[pl.ds(pl.multiple_of(p * 2 * heads, heads), heads), :] = lse[pl.ds(pl.multiple_of(p * heads, heads), heads), :]
        stats[pl.ds(pl.multiple_of((p * 2 + 1) * heads, heads), heads), :] = jnp.concatenate(sums, axis=0)

    for o_at in range(1, PLANE):
        plane_copy(last, o_at).start()
    own_copy(last).start()

    for n in range(3):
        own_copy(n).wait()
        for o_at in range(1, PLANE):
            arrival(n, o_at).wait_recv()
        for dz in range(1, HALO + 1):
            @pl.when(plane + dz < planes)
            def _():
                z_copy(n, dz).start()
    for path in routes:
        path.pass_on()
    own_copy(last).wait()
    own_copy(4).wait()
    own_copy(5).wait()
    for o_at in range(1, PLANE):
        arrival(last, o_at).wait_recv()
    for path in routes:
        path.wait_arrivals()
        path.wait_sends()
    for n in range(last + 1):
        for o_at in range(1, PLANE):
            plane_copy(n, o_at).wait_send()
    for n in range(3):
        for dz in range(1, HALO + 1):
            @pl.when(plane + dz < planes)
            def _():
                z_copy(n, dz).wait_send()

            @pl.when(plane >= dz)
            def _():
                z_copy(n, dz).wait_recv()


def gather(q, g, o, k, v, seg, lse, planes):
    rows = q.shape[0]
    span = rows * PLANE
    heads = lse.shape[0] // PLANE
    window = (HALO + 1) * span
    any_space = pl.BlockSpec(memory_space=pl.ANY)
    vmem = pl.BlockSpec(memory_space=pltpu.VMEM)
    return pl.pallas_call(
        functools.partial(gather_kernel, planes),
        out_shape=(
            jax.ShapeDtypeStruct((span, heads * D), q.dtype),
            jax.ShapeDtypeStruct((span, heads * D), g.dtype),
            jax.ShapeDtypeStruct((window, D), k.dtype),
            jax.ShapeDtypeStruct((window, D), v.dtype),
            jax.ShapeDtypeStruct((2 * heads, span), lse.dtype),
            jax.ShapeDtypeStruct((8, window), seg.dtype),
        ),
        in_specs=[any_space] * 5 + [vmem] * 2,
        out_specs=(any_space,) * 6,
        scratch_shapes=[
            pltpu.VMEM(o.shape, o.dtype),
            pltpu.VMEM(g.shape, g.dtype),
            pltpu.VMEM((2 * heads * PLANE, rows), jnp.float32),
            pltpu.VMEM((8, rows), jnp.int32),
            pltpu.VMEM((2, CHUNKS, PLANE_X - 1, rows, heads * D // CHUNKS), q.dtype),
            pltpu.SemaphoreType.DMA((2, CHUNKS, ROUTE_SEMS)),
            pltpu.SemaphoreType.DMA((2, CHUNKS, ROUTE_SEMS)),
            pltpu.SemaphoreType.DMA((4, PLANE - 1)),
            pltpu.SemaphoreType.DMA((4, PLANE - 1)),
            pltpu.SemaphoreType.DMA((3, HALO)),
            pltpu.SemaphoreType.DMA((3, HALO)),
            pltpu.SemaphoreType.DMA((8,)),
        ],
        compiler_params=pltpu.CompilerParams(
            collective_id=0, has_side_effects=True, vmem_limit_bytes=VMEM_LIMIT
        ),
        name="gather_plane",
    )(q, g, o, k, v, seg, lse)


def attend_kernel(
    seg, stats, q, g, k, v, dq, dk_halo, dv_halo, dk_own, dv_own, dk, dv, k_t, start
):
    i = pl.program_id(0)
    window = k.shape[0]
    span = dk_own.shape[0]
    own = window - span
    heads = q.shape[1] // D
    across = heads * BLOCK
    inv_root = 1.0 / math.sqrt(D)
    scale = inv_root * LOG2E

    @pl.when(i == 0)
    def _():
        dk[...] = jnp.zeros_like(dk)
        dv[...] = jnp.zeros_like(dv)
        k_t[...] = k[...].T
        ids = seg[...]
        at = lax.broadcasted_iota(jnp.int32, ids.shape, 1)
        plane = lax.axis_index("seq") // PLANE
        first = own - jnp.minimum(plane, HALO) * span
        begins = (ids != pltpu.roll(ids, 1, 1)) & (at > first)
        found = jnp.where(begins, at, first)
        step = 1
        while step < window:
            found = jnp.where(at >= step, jnp.maximum(found, pltpu.roll(found, step, 1)), found)
            step *= 2
        start[...] = found[:, own:]

    def stacked(ref):
        return jnp.concatenate([ref[:, h * D:(h + 1) * D] for h in range(heads)], axis=0)

    def in_line(first):
        return jnp.concatenate([stats[first + h:first + h + 1, :] for h in range(heads)], axis=1)

    q_rows, g_rows = stacked(q), stacked(g)
    lse_row = in_line(0) * LOG2E
    delta_row = in_line(heads)
    block_start = start[0:1, pl.ds(pl.multiple_of(i * BLOCK, BLOCK), BLOCK)]
    start_row = jnp.concatenate([block_start] * heads, axis=1)
    query_row = own + i * BLOCK + lax.rem(lax.broadcasted_iota(jnp.int32, (1, across), 1), BLOCK)

    def tile(masked, j, dq_t):
        there = pl.ds(pl.multiple_of(j * BLOCK, BLOCK), BLOCK)
        k_rows, v_rows = k[there, :], v[there, :]
        nt = (((1,), (1,)), ((), ()))
        scores = lax.dot_general(k_rows, q_rows, nt, preferred_element_type=jnp.float32)
        weights = jnp.exp2(scores * scale - lse_row)
        if masked:
            key_at = j * BLOCK + lax.broadcasted_iota(jnp.int32, (BLOCK, across), 0)
            weights = jnp.where((key_at >= start_row) & (key_at <= query_row), weights, 0.0)
        d_weights = lax.dot_general(v_rows, g_rows, nt, preferred_element_type=jnp.float32)
        dscore = (weights * (d_weights - delta_row)).astype(jnp.bfloat16)
        low = weights.astype(jnp.bfloat16)
        dv[there, :] += jnp.dot(low, g_rows, preferred_element_type=jnp.float32)
        dk[there, :] += jnp.dot(dscore, q_rows, preferred_element_type=jnp.float32)
        return dq_t + jnp.dot(k_t[:, there], dscore, preferred_element_type=jnp.float32)

    position = block_start.astype(jnp.float32)
    diagonal = own // BLOCK + i
    low_end = jnp.min(position).astype(jnp.int32) // BLOCK
    full = (jnp.max(position).astype(jnp.int32) + BLOCK - 1) // BLOCK
    full = jnp.clip(full, low_end, diagonal)
    dq_t = jnp.zeros((D, across), jnp.float32)
    dq_t = lax.fori_loop(low_end, full, functools.partial(tile, True), dq_t)
    dq_t = lax.fori_loop(full, diagonal, functools.partial(tile, False), dq_t)
    dq_t = tile(True, diagonal, dq_t)
    for h in range(heads):
        dq[:, h * D:(h + 1) * D] = (dq_t[:, h * BLOCK:(h + 1) * BLOCK].T * inv_root).astype(dq.dtype)

    @pl.when(i == pl.num_programs(0) - 1)
    def _():
        dk_halo[...] = (dk[:own, :] * inv_root).astype(dk_halo.dtype)
        dv_halo[...] = dv[:own, :].astype(dv_halo.dtype)
        dk_own[...] = dk[own:, :] * inv_root
        dv_own[...] = dv[own:, :]


def attend(q, g, k, v, stats, seg_win):
    span, wide = q.shape
    window = k.shape[0]
    own = window - span
    block = pl.BlockSpec((BLOCK, wide), lambda i: (i, 0))

    def whole(shape):
        return pl.BlockSpec(shape, lambda i: (0, 0))

    return pl.pallas_call(
        attend_kernel,
        grid=(span // BLOCK,),
        in_specs=[
            whole(seg_win.shape), pl.BlockSpec((stats.shape[0], BLOCK), lambda i: (0, i)),
            block, block, whole((window, D)), whole((window, D)),
        ],
        out_specs=[block, whole((own, D)), whole((own, D)), whole((span, D)), whole((span, D))],
        out_shape=(
            jax.ShapeDtypeStruct((span, wide), q.dtype),
            jax.ShapeDtypeStruct((own, D), jnp.bfloat16),
            jax.ShapeDtypeStruct((own, D), jnp.bfloat16),
            jax.ShapeDtypeStruct((span, D), jnp.float32),
            jax.ShapeDtypeStruct((span, D), jnp.float32),
        ),
        scratch_shapes=[
            pltpu.VMEM((window, D), jnp.float32),
            pltpu.VMEM((window, D), jnp.float32),
            pltpu.VMEM((D, window), jnp.bfloat16),
            pltpu.VMEM((8, span), jnp.int32),
        ],
        compiler_params=pltpu.CompilerParams(vmem_limit_bytes=VMEM_LIMIT),
        name="attend",
    )(seg_win, stats, q, g, k, v)


def scatter_kernel(
    planes, dq, dk_halo, dv_halo, dk_own, dv_own, grad_q, grad_k, grad_v,
    dk_in, dv_in, dk_low, dv_low, total, stage, r_send, r_recv, z_send, z_recv, last_send, last_recv, local,
):
    rows = grad_q.shape[0]
    span = rows * PLANE
    wide = dq.shape[1]
    me = lax.axis_index("seq")
    plane, rank = me // PLANE, lax.rem(me, PLANE)

    def cols(index, width):
        return pl.ds(pl.multiple_of(index * width, width), width)

    def z_copy(n, dz):
        halo, into = ((dk_halo, dk_in), (dv_halo, dv_in))[n]
        return pltpu.make_async_remote_copy(
            halo.at[pl.ds((HALO - dz) * span, span), :], into.at[dz - 1],
            z_send.at[n, dz - 1], z_recv.at[n, dz - 1],
            device_id=dev(me - dz * PLANE), device_id_type=MESH,
        )

    def route(c):
        narrow = wide // 2

        def source(p):
            return dq.at[cols(p, rows), pl.ds(c * narrow, narrow)]

        def target(s):
            return grad_q.at[:, pl.ds(pl.multiple_of(s * wide + c * narrow, narrow), narrow)]

        return Route(c == 0, plane, rank, source, target, stage.at[c], (r_send.at[c], r_recv.at[c]))

    routes = [route(c) for c in range(2)]

    def kv_copy(n, o, origin):
        low, out = ((dk_low, grad_k), (dv_low, grad_v))[n]
        peer = lax.rem(rank + o, PLANE)
        return pltpu.make_async_remote_copy(
            low.at[cols(peer, rows), :], out.at[:, cols(origin, D)], last_send.at[n, o - 1], last_recv.at[n, o - 1],
            device_id=dev(plane * PLANE + peer), device_id_type=MESH,
        )

    greet(me, plane, rank, planes)
    for n in range(2):
        for dz in range(1, HALO + 1):
            @pl.when(plane >= dz)
            def _():
                z_copy(n, dz).start()
    for path in routes:
        path.start_first()
    for path in routes:
        path.start_straight()
    own_q = pltpu.make_async_copy(dq.at[cols(rank, rows), :], grad_q.at[:, cols(rank, wide)], local.at[0])
    own_q.start()
    for path in routes:
        path.pass_on()
    own_kv = []
    for n in range(2):
        low, out, own, into = ((dk_low, grad_k, dk_own, dk_in), (dv_low, grad_v, dv_own, dv_in))[n]
        total[...] = own[...]
        for dz in range(1, HALO + 1):
            @pl.when(plane + dz < planes)
            def _():
                z_copy(n, dz).wait_recv()
                total[...] += into[dz - 1].astype(jnp.float32)
        low[...] = total[...].astype(low.dtype)
        for o in range(1, PLANE):
            kv_copy(n, o, rank).start()
        own_kv.append(pltpu.make_async_copy(low.at[cols(rank, rows), :], out.at[:, cols(rank, D)], local.at[1 + n]))
        own_kv[n].start()
    own_q.wait()
    for n in range(2):
        own_kv[n].wait()
        for dz in range(1, HALO + 1):
            @pl.when(plane >= dz)
            def _():
                z_copy(n, dz).wait_send()
    for path in routes:
        path.wait_arrivals()
        path.wait_sends()
    for o in range(1, PLANE):
        origin = lax.rem(rank + PLANE - o, PLANE)
        for n in range(2):
            kv_copy(n, o, origin).wait()


def scatter(dq, dk_halo, dv_halo, dk_own, dv_own, planes):
    span, wide = dq.shape
    rows = span // PLANE
    any_space = pl.BlockSpec(memory_space=pl.ANY)
    vmem = pl.BlockSpec(memory_space=pltpu.VMEM)
    return pl.pallas_call(
        functools.partial(scatter_kernel, planes),
        out_shape=(
            jax.ShapeDtypeStruct((rows, PLANE * wide), dq.dtype),
            jax.ShapeDtypeStruct((rows, PLANE * D), jnp.bfloat16),
            jax.ShapeDtypeStruct((rows, PLANE * D), jnp.bfloat16),
        ),
        in_specs=[any_space] * 3 + [vmem] * 2,
        out_specs=(any_space,) * 3,
        scratch_shapes=[
            pltpu.VMEM((HALO, span, D), jnp.bfloat16),
            pltpu.VMEM((HALO, span, D), jnp.bfloat16),
            pltpu.VMEM((span, D), jnp.bfloat16),
            pltpu.VMEM((span, D), jnp.bfloat16),
            pltpu.VMEM((span, D), jnp.float32),
            pltpu.VMEM((2, PLANE_X - 1, rows, wide // 2), dq.dtype),
            pltpu.SemaphoreType.DMA((2, ROUTE_SEMS)),
            pltpu.SemaphoreType.DMA((2, ROUTE_SEMS)),
            pltpu.SemaphoreType.DMA((2, HALO)),
            pltpu.SemaphoreType.DMA((2, HALO)),
            pltpu.SemaphoreType.DMA((2, PLANE - 1)),
            pltpu.SemaphoreType.DMA((2, PLANE - 1)),
            pltpu.SemaphoreType.DMA((3,)),
        ],
        compiler_params=pltpu.CompilerParams(
            collective_id=1, has_side_effects=True, vmem_limit_bytes=VMEM_LIMIT
        ),
        name="scatter_plane",
    )(dq, dk_halo, dv_halo, dk_own, dv_own)


def on_device(queries, keys, values, outputs, out_grad, lse, segments):
    planes = lax.axis_size("seq") // PLANE
    q, g, k, v, stats, seg_win = gather(
        queries, out_grad, outputs, keys, values, segments[None, :], lse, planes
    )
    return scatter(*attend(q, g, k, v, stats, seg_win), planes)


def solution(mesh):
    rows = P(("dp", "seq"), None)
    in_specs = (rows, rows, rows, rows, rows, P(None, ("dp", "seq")), P(("dp", "seq")))
    return jax.shard_map(
        on_device, mesh=mesh, in_specs=in_specs, out_specs=(rows, rows, rows), check_vma=False
    )
```

```python
import functools
import math

import jax
import jax.numpy as jnp
from jax import lax
from jax.experimental import pallas as pl
from jax.experimental.pallas import tpu as pltpu
from jax.sharding import PartitionSpec as P

D = 128
LOG2E = math.log2(math.e)
MESH = pl.DeviceIdType.MESH
PLANE = 8
PLANE_X = 4
HALO = 2
NEAR = 2
CHUNKS = 4
ROUTE_SEMS = 10
BLOCK = 256
VMEM_LIMIT = 60 * 1024 * 1024


def dev(index):
    return {"seq": index}


def greet(me, plane, rank, planes, reach):
    barrier = pltpu.get_barrier_semaphore()
    for o in range(1, PLANE):
        peer = plane * PLANE + lax.rem(rank + o, PLANE)
        pl.semaphore_signal(barrier, inc=1, device_id=dev(peer), device_id_type=MESH)
    count = PLANE - 1
    for dz in range(1, reach + 1):
        up = plane + dz < planes
        down = plane >= dz

        @pl.when(up)
        def _():
            pl.semaphore_signal(barrier, inc=1, device_id=dev(me + dz * PLANE), device_id_type=MESH)

        @pl.when(down)
        def _():
            pl.semaphore_signal(barrier, inc=1, device_id=dev(me - dz * PLANE), device_id_type=MESH)

        count = count + up.astype(jnp.int32) + down.astype(jnp.int32)
    pl.semaphore_wait(barrier, count)


class Route:
    def __init__(self, x_first, plane, rank, source, target, stage, sems):
        self.x_first, self.plane = x_first, plane
        self.y, self.x = rank // PLANE_X, lax.rem(rank, PLANE_X)
        self.source, self.target, self.stage = source, target, stage
        self.send, self.recv = sems

    def rank(self, dy, dx):
        y = self.y if dy == 0 else 1 - self.y
        return y * PLANE_X + lax.rem(self.x + dx + PLANE_X, PLANE_X)

    def copy(self, n, source, target, peer):
        return pltpu.make_async_remote_copy(
            source, target, self.send.at[n], self.recv.at[n],
            device_id=dev(self.plane * PLANE + peer), device_id_type=MESH,
        )

    def first_leg(self, dx):
        peer = self.rank(0, dx) if self.x_first else self.rank(1, 0)
        return self.copy(dx - 1, self.source(self.rank(1, dx)), self.stage.at[dx - 1], peer)

    def second_leg(self, dx):
        if self.x_first:
            origin, peer = self.rank(0, -dx), self.rank(1, 0)
        else:
            origin, peer = self.rank(1, 0), self.rank(0, dx)
        return self.copy(2 + dx, self.stage.at[dx - 1], self.target(origin), peer)

    def straight(self, dx):
        peer = self.rank(0, dx) if dx else self.rank(1, 0)
        return self.copy(6 + dx, self.source(peer), self.target(self.rank(0, 0)), peer)

    def start_first(self):
        for dx in range(1, PLANE_X):
            self.first_leg(dx).start()

    def start_straight(self):
        for dx in range(PLANE_X):
            self.straight(dx).start()

    def pass_on(self):
        for dx in range(1, PLANE_X):
            self.first_leg(dx).wait_recv()
            self.second_leg(dx).start()

    def wait_arrivals(self):
        for dx in range(PLANE_X):
            origin = self.rank(0, -dx) if dx else self.rank(1, 0)
            self.copy(6 + dx, self.target(origin), self.target(origin), origin).wait_recv()
        for dx in range(1, PLANE_X):
            origin = self.rank(1, -dx)
            self.copy(2 + dx, self.target(origin), self.target(origin), origin).wait_recv()

    def wait_sends(self):
        for dx in range(1, PLANE_X):
            self.first_leg(dx).wait_send()
            self.second_leg(dx).wait_send()
        for dx in range(PLANE_X):
            self.straight(dx).wait_send()


def tile_terms(k_rows, v_rows, q_rows, g_rows, lse_row, delta_row, visible):
    nt = (((1,), (1,)), ((), ()))
    scores = lax.dot_general(k_rows, q_rows, nt, preferred_element_type=jnp.float32)
    weights = jnp.exp2(scores * (LOG2E / math.sqrt(D)) - lse_row)
    if visible is not None:
        weights = jnp.where(visible(), weights, 0.0)
    d_weights = lax.dot_general(v_rows, g_rows, nt, preferred_element_type=jnp.float32)
    dscore = (weights * (d_weights - delta_row)).astype(jnp.bfloat16)
    return weights.astype(jnp.bfloat16), dscore


def begins_at(ids, first):
    at = lax.broadcasted_iota(jnp.int32, ids.shape, 1)
    begins = (ids != pltpu.roll(ids, 1, 1)) & (at > first)
    found = jnp.where(begins, at, first)
    step = 1
    while step < ids.shape[1]:
        found = jnp.where(at >= step, jnp.maximum(found, pltpu.roll(found, step, 1)), found)
        step *= 2
    return found


def gather_kernel(
    planes, q, g, o, k, v, seg, lse, q_all, g_all, k_win, v_win, dq_part, stats_all, seg_win, dk, dv,
    o_here, g_here, q_in, g_in, k_in, v_in, k_t, start, dq_t, stats, seg_here, stage,
    r_send, r_recv, send, recv, z_send, z_recv, local, chunk_out,
):
    rows = q.shape[0]
    span = rows * PLANE
    wide = q_in.shape[1]
    heads = wide // D
    me = lax.axis_index("seq")
    plane, rank = me // PLANE, lax.rem(me, PLANE)
    own = HALO * span
    narrow = wide // CHUNKS
    per_chunk = narrow // D
    across = per_chunk * BLOCK
    near = NEAR * BLOCK

    def part(index, width):
        return pl.ds(pl.multiple_of(index * width, width), width)

    def own_part(s):
        return pl.ds(pl.multiple_of(own + s * rows, rows), rows)

    pieces = [
        (lambda p: seg_here, lambda s: seg_win.at[:, own_part(s)]),
        (lambda p: k.at[:, part(p, D)], lambda s: k_win.at[own_part(s), :]),
        (lambda p: v.at[:, part(p, D)], lambda s: v_win.at[own_part(s), :]),
        (lambda p: stats.at[part(p, 2 * heads), :], lambda s: stats_all.at[:, part(s, rows)]),
        (lambda p: q.at[:, part(p, wide)], lambda s: q_in.at[part(s, rows), :]),
        (lambda p: g.at[:, part(p, wide)], lambda s: g_in.at[part(s, rows), :]),
    ]
    last = 3

    def routes(c):
        made = []
        for n, (array, gathered) in enumerate(((q, q_in), (g, g_in))):
            def source(p, array=array):
                return array.at[:, pl.ds(pl.multiple_of(p * wide + c * narrow, narrow), narrow)]

            def target(s, gathered=gathered):
                return gathered.at[part(s, rows), part(c, narrow)]

            made.append(Route(
                n == 0, plane, rank, source, target, stage.at[n, c], (r_send.at[n, c], r_recv.at[n, c])
            ))
        return made

    def own_copy(n):
        source, target = pieces[n]
        return pltpu.make_async_copy(source(rank), target(rank), local.at[n])

    def plane_copy(n, o):
        source, target = pieces[n]
        peer = lax.rem(rank + o, PLANE)
        return pltpu.make_async_remote_copy(
            source(peer), target(rank), send.at[n, o - 1], recv.at[n, o - 1],
            device_id=dev(plane * PLANE + peer), device_id_type=MESH,
        )

    def arrival(n, o):
        source, target = pieces[n]
        origin = lax.rem(rank + PLANE - o, PLANE)
        return pltpu.make_async_remote_copy(
            source(rank), target(origin), send.at[n, o - 1], recv.at[n, o - 1],
            device_id=dev(plane * PLANE + origin), device_id_type=MESH,
        )

    def z_copy(n, dz):
        held, there = pl.ds(own - (dz - 1) * span, span), pl.ds(own - dz * span, span)
        if n == 0:
            source, target = seg_win.at[:, held], seg_win.at[:, there]
        else:
            win = (k_win, v_win)[n - 1]
            source, target = win.at[held, :], win.at[there, :]
        return pltpu.make_async_remote_copy(
            source, target, z_send.at[n, dz - 1], z_recv.at[n, dz - 1],
            device_id=dev(me + PLANE), device_id_type=MESH,
        )

    def z_sends(dz):
        return (plane + 1 < planes) & (plane + 1 >= dz)

    def start_chunk(c):
        for path in routes(c):
            path.start_first()
        for path in routes(c):
            path.start_straight()

    def pass_on(c):
        for path in routes(c):
            path.pass_on()

    def put_copy(n, c):
        here = part(c, narrow)
        if n == 0:
            return pltpu.make_async_copy(q_in.at[:, here], q_all.at[:, here], chunk_out.at[n, c])
        if n == 1:
            return pltpu.make_async_copy(g_in.at[:, here], g_all.at[:, here], chunk_out.at[n, c])
        here = part(c, across)
        return pltpu.make_async_copy(dq_t.at[:, here], dq_part.at[:, here], chunk_out.at[n, c])

    load_o = pltpu.make_async_copy(o, o_here, local.at[6])
    load_g = pltpu.make_async_copy(g, g_here, local.at[7])
    load_o.start()
    load_g.start()
    seg_here[...] = jnp.broadcast_to(seg[...], seg_here.shape)
    greet(me, plane, rank, planes, 1)
    for n in range(last):
        for o_at in range(1, PLANE):
            plane_copy(n, o_at).start()
        own_copy(n).start()
    start_chunk(0)
    start_chunk(1)
    own_copy(4).start()
    own_copy(5).start()

    load_o.wait()
    load_g.wait()

    @pl.loop(0, PLANE)
    def _(p):
        sums = []
        for h in range(heads):
            features = pl.ds(pl.multiple_of(p * wide + h * D, D), D)
            product = o_here[:, features].astype(jnp.float32) * g_here[:, features].astype(jnp.float32)
            sums.append(jnp.sum(product.T, axis=0, keepdims=True))
        stats[part(p * 2, heads), :] = lse[part(p, heads), :]
        stats[part(p * 2 + 1, heads), :] = jnp.concatenate(sums, axis=0)

    for o_at in range(1, PLANE):
        plane_copy(last, o_at).start()
    own_copy(last).start()

    for n in range(3):
        own_copy(n).wait()
        for o_at in range(1, PLANE):
            arrival(n, o_at).wait_recv()
        @pl.when(z_sends(1))
        def _():
            z_copy(n, 1).start()

    load_k = pltpu.make_async_copy(k_win.at[pl.ds(own, span), :], k_in.at[pl.ds(near, span), :], local.at[6])
    load_v = pltpu.make_async_copy(v_win.at[pl.ds(own, span), :], v_in.at[pl.ds(near, span), :], local.at[7])
    load_k.start()
    load_v.start()
    pass_on(0)
    dk[...] = jnp.zeros_like(dk)
    dv[...] = jnp.zeros_like(dv)
    load_k.wait()
    load_v.wait()
    for n in range(3):
        @pl.when(plane >= 1)
        def _():
            z_copy(n, 1).wait_recv()

        @pl.when(z_sends(2))
        def _():
            z_copy(n, 2).start()

    load_k = pltpu.make_async_copy(k_win.at[pl.ds(own - near, near), :], k_in.at[pl.ds(0, near), :], local.at[6])
    load_v = pltpu.make_async_copy(v_win.at[pl.ds(own - near, near), :], v_in.at[pl.ds(0, near), :], local.at[7])

    @pl.when(plane >= 1)
    def _():
        load_k.start()
        load_v.start()
        load_k.wait()
        load_v.wait()

    @pl.when(plane < 1)
    def _():
        k_in[:near, :] = jnp.zeros((near, D), k_in.dtype)
        v_in[:near, :] = jnp.zeros((near, D), v_in.dtype)

    known = jnp.where(plane >= 1, 0, near)
    start[...] = begins_at(seg_win[:, pl.ds(own - near, near + span)], known)[:, near:]
    k_t[...] = k_in[...].T
    own_copy(last).wait()
    own_copy(4).wait()
    own_copy(5).wait()
    for o_at in range(1, PLANE):
        arrival(last, o_at).wait_recv()

    @pl.loop(0, CHUNKS)
    def _(c):
        @pl.when(c + 2 < CHUNKS)
        def _():
            start_chunk(c + 2)

        @pl.when(c + 1 < CHUNKS)
        def _():
            pass_on(c + 1)

        for path in routes(c):
            path.wait_arrivals()
        put_copy(0, c).start()
        put_copy(1, c).start()

        blocks = span // BLOCK
        operands = []
        for i in range(blocks):
            here = pl.ds(i * BLOCK, BLOCK)

            def stacked(ref, here=here):
                return jnp.concatenate(
                    [ref[here, pl.ds(pl.multiple_of(c * narrow + h * D, D), D)] for h in range(per_chunk)], axis=0
                )

            def in_line(first, here=here):
                return jnp.concatenate(
                    [stats_all[pl.ds(first + c * per_chunk + h, 1), here] for h in range(per_chunk)], axis=1
                )

            start_row = jnp.concatenate([start[0:1, here]] * per_chunk, axis=1)
            operands.append((stacked(q_in), stacked(g_in), in_line(0) * LOG2E, in_line(heads), start_row))
        totals = [jnp.zeros((D, across), jnp.float32) for _ in range(blocks)]
        down = lax.broadcasted_iota(jnp.int32, (BLOCK, across), 0)
        query_at = lax.rem(lax.broadcasted_iota(jnp.int32, (1, across), 1), BLOCK)
        for back in range(blocks + NEAR):
            for i in range(blocks):
                j = NEAR + i - back
                if j < 0:
                    continue
                there = pl.ds(j * BLOCK, BLOCK)
                q_rows, g_rows, lse_row, delta_row, start_row = operands[i]

                def visible(j=j, back=back, start_row=start_row):
                    seen = down >= start_row - j * BLOCK
                    return seen & (down <= query_at) if back == 0 else seen

                low, dscore = tile_terms(k_in[there, :], v_in[there, :], q_rows, g_rows, lse_row, delta_row, visible)
                dv[there, :] += jnp.dot(low, g_rows, preferred_element_type=jnp.float32)
                dk[there, :] += jnp.dot(dscore, q_rows, preferred_element_type=jnp.float32)
                totals[i] += jnp.dot(k_t[:, there], dscore, preferred_element_type=jnp.float32)
        for i in range(blocks):
            dq_t[pl.ds(i * D, D), part(c, across)] = totals[i]

        put_copy(2, c).start()

    for c in range(CHUNKS):
        for path in routes(c):
            path.wait_sends()
        for n in range(3):
            put_copy(n, c).wait()
    for n in range(last + 1):
        for o_at in range(1, PLANE):
            plane_copy(n, o_at).wait_send()
    for n in range(3):
        for dz in range(1, HALO + 1):
            @pl.when(z_sends(dz))
            def _():
                z_copy(n, dz).wait_send()

        @pl.when(plane >= 2)
        def _():
            z_copy(n, 2).wait_recv()


def gather(q, g, o, k, v, seg, lse, planes):
    rows = q.shape[0]
    span = rows * PLANE
    heads = lse.shape[0] // PLANE
    wide = heads * D
    window = (HALO + 1) * span
    near = NEAR * BLOCK
    part_shape = (span // BLOCK * D, heads * BLOCK)
    any_space = pl.BlockSpec(memory_space=pl.ANY)
    vmem = pl.BlockSpec(memory_space=pltpu.VMEM)
    return pl.pallas_call(
        functools.partial(gather_kernel, planes),
        out_shape=(
            jax.ShapeDtypeStruct((span, wide), q.dtype),
            jax.ShapeDtypeStruct((span, wide), g.dtype),
            jax.ShapeDtypeStruct((window, D), k.dtype),
            jax.ShapeDtypeStruct((window, D), v.dtype),
            jax.ShapeDtypeStruct(part_shape, jnp.float32),
            jax.ShapeDtypeStruct((2 * heads, span), lse.dtype),
            jax.ShapeDtypeStruct((8, window), seg.dtype),
            jax.ShapeDtypeStruct((near + span, D), jnp.float32),
            jax.ShapeDtypeStruct((near + span, D), jnp.float32),
        ),
        in_specs=[any_space] * 5 + [vmem] * 2,
        out_specs=(any_space,) * 5 + (vmem,) * 4,
        scratch_shapes=[
            pltpu.VMEM(o.shape, o.dtype),
            pltpu.VMEM(g.shape, g.dtype),
            pltpu.VMEM((span, wide), q.dtype),
            pltpu.VMEM((span, wide), g.dtype),
            pltpu.VMEM((near + span, D), k.dtype),
            pltpu.VMEM((near + span, D), v.dtype),
            pltpu.VMEM((D, near + span), k.dtype),
            pltpu.VMEM((8, span), jnp.int32),
            pltpu.VMEM(part_shape, jnp.float32),
            pltpu.VMEM((2 * heads * PLANE, rows), jnp.float32),
            pltpu.VMEM((8, rows), jnp.int32),
            pltpu.VMEM((2, CHUNKS, PLANE_X - 1, rows, wide // CHUNKS), q.dtype),
            pltpu.SemaphoreType.DMA((2, CHUNKS, ROUTE_SEMS)),
            pltpu.SemaphoreType.DMA((2, CHUNKS, ROUTE_SEMS)),
            pltpu.SemaphoreType.DMA((4, PLANE - 1)),
            pltpu.SemaphoreType.DMA((4, PLANE - 1)),
            pltpu.SemaphoreType.DMA((3, HALO)),
            pltpu.SemaphoreType.DMA((3, HALO)),
            pltpu.SemaphoreType.DMA((8,)),
            pltpu.SemaphoreType.DMA((3, CHUNKS)),
        ],
        compiler_params=pltpu.CompilerParams(
            collective_id=0, has_side_effects=True, vmem_limit_bytes=VMEM_LIMIT
        ),
        name="gather_plane",
    )(q, g, o, k, v, seg, lse)


def attend_kernel(seg, stats, q, g, k, v, dq_part, dk_near, dv_near, dq, dk_halo, dv_halo, dk, dv, k_t, start):
    i = pl.program_id(0)
    own = k.shape[0]
    span = own // HALO
    heads = q.shape[1] // D
    across = heads * BLOCK
    inv_root = 1.0 / math.sqrt(D)
    halo_end = own // BLOCK - NEAR

    @pl.when(i == 0)
    def _():
        far = halo_end * BLOCK
        dk[:far, :] = jnp.zeros((far, D), jnp.float32)
        dv[:far, :] = jnp.zeros((far, D), jnp.float32)
        dk[far:, :] = dk_near[...]
        dv[far:, :] = dv_near[...]
        k_t[...] = k[...].T
        plane = lax.axis_index("seq") // PLANE
        found = begins_at(seg[...], own - jnp.minimum(plane, HALO) * span)
        start[...] = found[:, own:]

    block_start = start[0:1, pl.ds(pl.multiple_of(i * BLOCK, BLOCK), BLOCK)]
    position = block_start.astype(jnp.float32)
    low_end = jnp.minimum(jnp.min(position).astype(jnp.int32) // BLOCK, halo_end)
    full = (jnp.max(position).astype(jnp.int32) + BLOCK - 1) // BLOCK
    full = jnp.clip(full, low_end, halo_end)

    def put(total):
        for h in range(heads):
            dq[:, h * D:(h + 1) * D] = (total[:, h * BLOCK:(h + 1) * BLOCK].T * inv_root).astype(dq.dtype)

    @pl.when(low_end == halo_end)
    def _():
        put(dq_part)

    @pl.when(low_end < halo_end)
    def _():
        def stacked(ref):
            return jnp.concatenate([ref[:, h * D:(h + 1) * D] for h in range(heads)], axis=0)

        def in_line(first):
            return jnp.concatenate([stats[first + h:first + h + 1, :] for h in range(heads)], axis=1)

        q_rows, g_rows = stacked(q), stacked(g)
        lse_row = in_line(0) * LOG2E
        delta_row = in_line(heads)
        start_row = jnp.concatenate([block_start] * heads, axis=1)

        def tile(masked, j, total):
            there = pl.ds(pl.multiple_of(j * BLOCK, BLOCK), BLOCK)

            def visible():
                return j * BLOCK + lax.broadcasted_iota(jnp.int32, (BLOCK, across), 0) >= start_row

            low, dscore = tile_terms(
                k[there, :], v[there, :], q_rows, g_rows, lse_row, delta_row, visible if masked else None
            )
            dv[there, :] += jnp.dot(low, g_rows, preferred_element_type=jnp.float32)
            dk[there, :] += jnp.dot(dscore, q_rows, preferred_element_type=jnp.float32)
            return total + jnp.dot(k_t[:, there], dscore, preferred_element_type=jnp.float32)

        total = lax.fori_loop(low_end, full, functools.partial(tile, True), dq_part[...])
        put(lax.fori_loop(full, halo_end, functools.partial(tile, False), total))

    @pl.when(i == pl.num_programs(0) - 1)
    def _():
        dk_halo[...] = (dk[...] * inv_root).astype(dk_halo.dtype)
        dv_halo[...] = dv[...].astype(dv_halo.dtype)


def attend(q, g, k, v, dq_part, dk, dv, stats, seg_win):
    span, wide = q.shape
    window = k.shape[0]
    own = window - span
    near = NEAR * BLOCK
    block = pl.BlockSpec((BLOCK, wide), lambda i: (i, 0))

    def whole(shape):
        return pl.BlockSpec(shape, lambda i: (0, 0))

    return pl.pallas_call(
        attend_kernel,
        grid=(span // BLOCK,),
        in_specs=[
            whole(seg_win.shape), pl.BlockSpec((stats.shape[0], BLOCK), lambda i: (0, i)),
            block, block, whole((own, D)), whole((own, D)),
            pl.BlockSpec((D, dq_part.shape[1]), lambda i: (i, 0)), whole((near, D)), whole((near, D)),
        ],
        out_specs=[block, whole((own, D)), whole((own, D))],
        out_shape=(
            jax.ShapeDtypeStruct((span, wide), q.dtype),
            jax.ShapeDtypeStruct((own, D), jnp.bfloat16),
            jax.ShapeDtypeStruct((own, D), jnp.bfloat16),
        ),
        scratch_shapes=[
            pltpu.VMEM((own, D), jnp.float32),
            pltpu.VMEM((own, D), jnp.float32),
            pltpu.VMEM((D, own), jnp.bfloat16),
            pltpu.VMEM((8, span), jnp.int32),
        ],
        compiler_params=pltpu.CompilerParams(vmem_limit_bytes=VMEM_LIMIT),
        name="attend",
    )(seg_win, stats, q, g, k, v, dq_part, dk, dv)


def scatter_kernel(
    planes, dq, dk_halo, dv_halo, dk_own, dv_own, grad_q, grad_k, grad_v,
    dk_in, dv_in, dk_low, dv_low, total, stage, r_send, r_recv, z_send, z_recv, last_send, last_recv, local,
):
    rows = grad_q.shape[0]
    span = rows * PLANE
    wide = dq.shape[1]
    me = lax.axis_index("seq")
    plane, rank = me // PLANE, lax.rem(me, PLANE)

    def cols(index, width):
        return pl.ds(pl.multiple_of(index * width, width), width)

    def z_copy(n, dz):
        halo, into = ((dk_halo, dk_in), (dv_halo, dv_in))[n]
        return pltpu.make_async_remote_copy(
            halo.at[pl.ds((HALO - dz) * span, span), :], into.at[dz - 1],
            z_send.at[n, dz - 1], z_recv.at[n, dz - 1],
            device_id=dev(me - dz * PLANE), device_id_type=MESH,
        )

    def route(c):
        narrow = wide // CHUNKS

        def source(p):
            return dq.at[cols(p, rows), pl.ds(c * narrow, narrow)]

        def target(s):
            return grad_q.at[:, pl.ds(pl.multiple_of(s * wide + c * narrow, narrow), narrow)]

        return Route(c % 2 == 0, plane, rank, source, target, stage.at[c], (r_send.at[c], r_recv.at[c]))

    routes = [route(c) for c in range(CHUNKS)]

    def kv_copy(n, o, origin):
        low, out = ((dk_low, grad_k), (dv_low, grad_v))[n]
        peer = lax.rem(rank + o, PLANE)
        return pltpu.make_async_remote_copy(
            low.at[cols(peer, rows), :], out.at[:, cols(origin, D)], last_send.at[n, o - 1], last_recv.at[n, o - 1],
            device_id=dev(plane * PLANE + peer), device_id_type=MESH,
        )

    greet(me, plane, rank, planes, HALO)
    for n in range(2):
        for dz in range(1, HALO + 1):
            @pl.when(plane >= dz)
            def _():
                z_copy(n, dz).start()
    def begin(c):
        routes[c].start_first()
        routes[c].start_straight()

    begin(0)
    begin(1)
    own_q = pltpu.make_async_copy(dq.at[cols(rank, rows), :], grad_q.at[:, cols(rank, wide)], local.at[0])
    own_q.start()
    for c in range(CHUNKS):
        routes[c].pass_on()
        if c + 2 < CHUNKS:
            begin(c + 2)
    own_kv = []
    for n in range(2):
        low, out, own, into = ((dk_low, grad_k, dk_own, dk_in), (dv_low, grad_v, dv_own, dv_in))[n]
        total[...] = own[pl.ds(own.shape[0] - span, span), :] * (1.0 / math.sqrt(D) if n == 0 else 1.0)
        for dz in range(1, HALO + 1):
            @pl.when(plane + dz < planes)
            def _():
                z_copy(n, dz).wait_recv()
                total[...] += into[dz - 1].astype(jnp.float32)
        low[...] = total[...].astype(low.dtype)
        for o in range(1, PLANE):
            kv_copy(n, o, rank).start()
        own_kv.append(pltpu.make_async_copy(low.at[cols(rank, rows), :], out.at[:, cols(rank, D)], local.at[1 + n]))
        own_kv[n].start()
    own_q.wait()
    for n in range(2):
        own_kv[n].wait()
        for dz in range(1, HALO + 1):
            @pl.when(plane >= dz)
            def _():
                z_copy(n, dz).wait_send()
    for path in routes:
        path.wait_arrivals()
        path.wait_sends()
    for o in range(1, PLANE):
        origin = lax.rem(rank + PLANE - o, PLANE)
        for n in range(2):
            kv_copy(n, o, origin).wait()


def scatter(dq, dk_halo, dv_halo, dk_own, dv_own, planes):
    span, wide = dq.shape
    rows = span // PLANE
    any_space = pl.BlockSpec(memory_space=pl.ANY)
    vmem = pl.BlockSpec(memory_space=pltpu.VMEM)
    return pl.pallas_call(
        functools.partial(scatter_kernel, planes),
        out_shape=(
            jax.ShapeDtypeStruct((rows, PLANE * wide), dq.dtype),
            jax.ShapeDtypeStruct((rows, PLANE * D), jnp.bfloat16),
            jax.ShapeDtypeStruct((rows, PLANE * D), jnp.bfloat16),
        ),
        in_specs=[any_space] * 3 + [vmem] * 2,
        out_specs=(any_space,) * 3,
        scratch_shapes=[
            pltpu.VMEM((HALO, span, D), jnp.bfloat16),
            pltpu.VMEM((HALO, span, D), jnp.bfloat16),
            pltpu.VMEM((span, D), jnp.bfloat16),
            pltpu.VMEM((span, D), jnp.bfloat16),
            pltpu.VMEM((span, D), jnp.float32),
            pltpu.VMEM((CHUNKS, PLANE_X - 1, rows, wide // CHUNKS), dq.dtype),
            pltpu.SemaphoreType.DMA((CHUNKS, ROUTE_SEMS)),
            pltpu.SemaphoreType.DMA((CHUNKS, ROUTE_SEMS)),
            pltpu.SemaphoreType.DMA((2, HALO)),
            pltpu.SemaphoreType.DMA((2, HALO)),
            pltpu.SemaphoreType.DMA((2, PLANE - 1)),
            pltpu.SemaphoreType.DMA((2, PLANE - 1)),
            pltpu.SemaphoreType.DMA((3,)),
        ],
        compiler_params=pltpu.CompilerParams(
            collective_id=1, has_side_effects=True, vmem_limit_bytes=VMEM_LIMIT
        ),
        name="scatter_plane",
    )(dq, dk_halo, dv_halo, dk_own, dv_own)


def on_device(queries, keys, values, outputs, out_grad, lse, segments):
    planes = lax.axis_size("seq") // PLANE
    q, g, k, v, dq_part, stats, seg_win, dk, dv = gather(
        queries, out_grad, outputs, keys, values, segments[None, :], lse, planes
    )
    return scatter(*attend(q, g, k, v, dq_part, dk, dv, stats, seg_win), dk, dv, planes)


def solution(mesh):
    rows = P(("dp", "seq"), None)
    in_specs = (rows, rows, rows, rows, rows, P(None, ("dp", "seq")), P(("dp", "seq")))
    return jax.shard_map(
        on_device, mesh=mesh, in_specs=in_specs, out_specs=(rows, rows, rows), check_vma=False
    )
```

```python
import functools
import math

import jax
import jax.numpy as jnp
from jax import lax
from jax.experimental import pallas as pl
from jax.experimental.pallas import tpu as pltpu
from jax.sharding import PartitionSpec as P

D = 128
LOG2E = math.log2(math.e)
MESH = pl.DeviceIdType.MESH
PLANE = 8
PLANE_X = 4
HALO = 2
CHUNKS = 4
WHOLE = 2
ROUTE_SEMS = 10
BLOCK = 256
VMEM_LIMIT = 60 * 1024 * 1024


def dev(index):
    return {"seq": index}


def greet(me, plane, rank, planes, reach):
    barrier = pltpu.get_barrier_semaphore()
    for o in range(1, PLANE):
        peer = plane * PLANE + lax.rem(rank + o, PLANE)
        pl.semaphore_signal(barrier, inc=1, device_id=dev(peer), device_id_type=MESH)
    count = PLANE - 1
    for dz in range(1, reach + 1):
        up = plane + dz < planes
        down = plane >= dz

        @pl.when(up)
        def _():
            pl.semaphore_signal(barrier, inc=1, device_id=dev(me + dz * PLANE), device_id_type=MESH)

        @pl.when(down)
        def _():
            pl.semaphore_signal(barrier, inc=1, device_id=dev(me - dz * PLANE), device_id_type=MESH)

        count = count + up.astype(jnp.int32) + down.astype(jnp.int32)
    pl.semaphore_wait(barrier, count)


class Route:
    def __init__(self, x_first, plane, rank, source, target, stage, sems):
        self.x_first, self.plane = x_first, plane
        self.y, self.x = rank // PLANE_X, lax.rem(rank, PLANE_X)
        self.source, self.target, self.stage = source, target, stage
        self.send, self.recv = sems

    def rank(self, dy, dx):
        y = self.y if dy == 0 else 1 - self.y
        return y * PLANE_X + lax.rem(self.x + dx + PLANE_X, PLANE_X)

    def copy(self, n, source, target, peer):
        return pltpu.make_async_remote_copy(
            source, target, self.send.at[n], self.recv.at[n],
            device_id=dev(self.plane * PLANE + peer), device_id_type=MESH,
        )

    def first_leg(self, dx):
        peer = self.rank(0, dx) if self.x_first else self.rank(1, 0)
        return self.copy(dx - 1, self.source(self.rank(1, dx)), self.stage.at[dx - 1], peer)

    def second_leg(self, dx):
        if self.x_first:
            origin, peer = self.rank(0, -dx), self.rank(1, 0)
        else:
            origin, peer = self.rank(1, 0), self.rank(0, dx)
        return self.copy(2 + dx, self.stage.at[dx - 1], self.target(origin), peer)

    def straight(self, dx):
        peer = self.rank(0, dx) if dx else self.rank(1, 0)
        return self.copy(6 + dx, self.source(peer), self.target(self.rank(0, 0)), peer)

    def start_first(self):
        for dx in range(1, PLANE_X):
            self.first_leg(dx).start()

    def start_straight(self):
        for dx in range(PLANE_X):
            self.straight(dx).start()

    def pass_on(self):
        for dx in range(1, PLANE_X):
            self.first_leg(dx).wait_recv()
            self.second_leg(dx).start()

    def wait_arrivals(self):
        for dx in range(PLANE_X):
            origin = self.rank(0, -dx) if dx else self.rank(1, 0)
            self.copy(6 + dx, self.target(origin), self.target(origin), origin).wait_recv()
        for dx in range(1, PLANE_X):
            origin = self.rank(1, -dx)
            self.copy(2 + dx, self.target(origin), self.target(origin), origin).wait_recv()

    def wait_sends(self):
        for dx in range(1, PLANE_X):
            self.first_leg(dx).wait_send()
            self.second_leg(dx).wait_send()
        for dx in range(PLANE_X):
            self.straight(dx).wait_send()


def tile_terms(k_rows, v_rows, q_rows, g_rows, lse_row, delta_row, visible):
    nt = (((1,), (1,)), ((), ()))
    scores = lax.dot_general(k_rows, q_rows, nt, preferred_element_type=jnp.float32)
    weights = jnp.exp2(scores * (LOG2E / math.sqrt(D)) - lse_row)
    if visible is not None:
        weights = jnp.where(visible(), weights, 0.0)
    d_weights = lax.dot_general(v_rows, g_rows, nt, preferred_element_type=jnp.float32)
    dscore = (weights * (d_weights - delta_row)).astype(jnp.bfloat16)
    return weights.astype(jnp.bfloat16), dscore


def begins_at(ids, first):
    at = lax.broadcasted_iota(jnp.int32, ids.shape, 1)
    begins = (ids != pltpu.roll(ids, 1, 1)) & (at > first)
    found = jnp.where(begins, at, first)
    step = 1
    while step < ids.shape[1]:
        found = jnp.where(at >= step, jnp.maximum(found, pltpu.roll(found, step, 1)), found)
        step *= 2
    return found


def kernel(
    planes, q, g, o, k, v, seg, lse, grad_q, grad_k, grad_v,
    o_here, g_here, q_in, g_in, k_in, v_in, k_t, start, seg_here, seg_win, stats, stats_in,
    dk, dv, dq_t, dq_low, far_out, far_in, near_out, near_in, low, stage, stage_back,
    r_send, r_recv, b_send, b_recv, send, recv, kv_send, kv_recv, z_send, z_recv, local,
):
    rows = q.shape[0]
    span = rows * PLANE
    wide = q_in.shape[1]
    heads = wide // D
    me = lax.axis_index("seq")
    plane, rank = me // PLANE, lax.rem(me, PLANE)
    own = HALO * span
    blocks = span // BLOCK
    narrow = wide // CHUNKS
    per_chunk = narrow // D
    across = per_chunk * BLOCK
    inv_root = 1.0 / math.sqrt(D)

    def part(index, width):
        return pl.ds(pl.multiple_of(index * width, width), width)

    def own_part(s):
        return pl.ds(pl.multiple_of(own + s * rows, rows), rows)

    pieces = [
        (lambda p: seg_here, lambda s: seg_win.at[:, own_part(s)]),
        (lambda p: k.at[:, part(p, D)], lambda s: k_in.at[own_part(s), :]),
        (lambda p: v.at[:, part(p, D)], lambda s: v_in.at[own_part(s), :]),
        (lambda p: stats.at[part(p, 2 * heads), :], lambda s: stats_in.at[:, part(s, rows)]),
        (lambda p: q.at[:, part(p, wide)], lambda s: q_in.at[part(s, rows), :]),
        (lambda p: g.at[:, part(p, wide)], lambda s: g_in.at[part(s, rows), :]),
    ]
    last = 3

    def routes(c):
        made = []
        for n, (array, gathered) in enumerate(((q, q_in), (g, g_in))):
            def source(p, array=array):
                return array.at[:, pl.ds(pl.multiple_of(p * wide + c * narrow, narrow), narrow)]

            def target(s, gathered=gathered):
                return gathered.at[part(s, rows), part(c, narrow)]

            made.append(Route(
                n == 0, plane, rank, source, target, stage.at[n, c], (r_send.at[n, c], r_recv.at[n, c])
            ))
        return made

    def route_back(c):
        def source(p):
            return dq_low.at[part(p, rows), pl.ds(c * narrow, narrow)]

        def target(s):
            return grad_q.at[:, pl.ds(pl.multiple_of(s * wide + c * narrow, narrow), narrow)]

        return Route(c % 2 == 0, plane, rank, source, target, stage_back.at[c], (b_send.at[c], b_recv.at[c]))

    back = [route_back(c) for c in range(CHUNKS)]

    def own_copy(n):
        source, target = pieces[n]
        return pltpu.make_async_copy(source(rank), target(rank), local.at[n])

    def plane_copy(n, o):
        source, target = pieces[n]
        peer = lax.rem(rank + o, PLANE)
        return pltpu.make_async_remote_copy(
            source(peer), target(rank), send.at[n, o - 1], recv.at[n, o - 1],
            device_id=dev(plane * PLANE + peer), device_id_type=MESH,
        )

    def arrival(n, o):
        source, target = pieces[n]
        origin = lax.rem(rank + PLANE - o, PLANE)
        return pltpu.make_async_remote_copy(
            source(rank), target(origin), send.at[n, o - 1], recv.at[n, o - 1],
            device_id=dev(plane * PLANE + origin), device_id_type=MESH,
        )

    def kv_copy(n, o, origin):
        peer = lax.rem(rank + o, PLANE)
        return pltpu.make_async_remote_copy(
            low.at[n, part(peer, rows), :], (grad_k, grad_v)[n].at[:, part(origin, D)],
            kv_send.at[n, o - 1], kv_recv.at[n, o - 1],
            device_id=dev(plane * PLANE + peer), device_id_type=MESH,
        )

    def z_copy(n, source, target, planes_on):
        return pltpu.make_async_remote_copy(
            source, target, z_send.at[n], z_recv.at[n],
            device_id=dev(me + planes_on * PLANE), device_id_type=MESH,
        )

    def seg_copy(dz):
        return z_copy(dz - 1, seg_win.at[:, pl.ds(own, span)], seg_win.at[:, pl.ds(own - dz * span, span)], dz)

    def halo_copy(n, dz):
        win = (k_in, v_in)[n]
        held, there = pl.ds(own - (dz - 1) * span, span), pl.ds(own - dz * span, span)
        return z_copy(2 * dz + n, win.at[held, :], win.at[there, :], 1)

    def far_copy(n):
        return z_copy(6 + n, far_out.at[n], far_in.at[n], -1)

    def near_copy(n):
        return z_copy(8 + n, near_out.at[n], near_in.at[n], -1)

    def start_chunk(c):
        for path in routes(c):
            path.start_first()
        for path in routes(c):
            path.start_straight()

    def pass_on(c):
        for path in routes(c):
            path.pass_on()

    def start_back(c):
        back[c].start_first()
        back[c].start_straight()

    def transpose_keys(dz):
        held = pl.ds(own - dz * span, span)
        k_t[:, held] = k_in[held, :].T

    def take_halo(dz):
        held = pl.ds(own - dz * span, span)

        @pl.when(plane >= dz)
        def _():
            for n in range(2):
                halo_copy(n, dz).wait_recv()

        @pl.when(plane < dz)
        def _():
            k_in[held, :] = jnp.zeros((span, D), k_in.dtype)
            v_in[held, :] = jnp.zeros((span, D), v_in.dtype)

        if dz < HALO:
            @pl.when((plane >= dz) & (plane + 1 < planes))
            def _():
                for n in range(2):
                    halo_copy(n, dz + 1).start()
        transpose_keys(dz)

    def tiles(c, dz, first):
        operands = []
        for i in range(blocks):
            here = pl.ds(i * BLOCK, BLOCK)

            def stacked(ref, here=here):
                return jnp.concatenate(
                    [ref[here, pl.ds(pl.multiple_of(c * narrow + h * D, D), D)] for h in range(per_chunk)], axis=0
                )

            def in_line(at, here=here):
                return jnp.concatenate(
                    [stats_in[pl.ds(at + c * per_chunk + h, 1), here] for h in range(per_chunk)], axis=1
                )

            start_row = jnp.concatenate([start[0:1, here]] * per_chunk, axis=1)
            operands.append((stacked(q_in), stacked(g_in), in_line(0) * LOG2E, in_line(heads), start_row))
        totals = [None] * blocks
        down = lax.broadcasted_iota(jnp.int32, (BLOCK, across), 0)
        query_at = lax.rem(lax.broadcasted_iota(jnp.int32, (1, across), 1), BLOCK)
        for before in range(HALO * blocks + 1):
            for i in range(blocks):
                j = HALO * blocks + i - before
                if j // blocks != HALO - dz:
                    continue
                there = pl.ds(j * BLOCK, BLOCK)
                q_rows, g_rows, lse_row, delta_row, start_row = operands[i]

                def visible(j=j, before=before, start_row=start_row):
                    seen = down >= start_row - j * BLOCK
                    return seen & (down <= query_at) if before == 0 else seen

                weights, dscore = tile_terms(
                    k_in[there, :], v_in[there, :], q_rows, g_rows, lse_row, delta_row, visible
                )
                dv[there, :] += jnp.dot(weights, g_rows, preferred_element_type=jnp.float32)
                dk[there, :] += jnp.dot(dscore, q_rows, preferred_element_type=jnp.float32)
                term = jnp.dot(k_t[:, there], dscore, preferred_element_type=jnp.float32)
                totals[i] = term if totals[i] is None else totals[i] + term
        for i in range(blocks):
            if first:
                dq_t[pl.ds(i * D, D), part(c, across)] = totals[i]
            else:
                dq_t[pl.ds(i * D, D), part(c, across)] += totals[i]

    def finish_queries(c):
        for i in range(blocks):
            for h in range(per_chunk):
                total = dq_t[pl.ds(i * D, D), pl.ds(pl.multiple_of(c * across + h * BLOCK, BLOCK), BLOCK)]
                dq_low[pl.ds(i * BLOCK, BLOCK), pl.ds(pl.multiple_of(c * narrow + h * D, D), D)] = (
                    total.T * inv_root
                ).astype(dq_low.dtype)

    load_o = pltpu.make_async_copy(o, o_here, local.at[6])
    load_g = pltpu.make_async_copy(g, g_here, local.at[7])
    load_o.start()
    load_g.start()
    seg_here[...] = jnp.broadcast_to(seg[...], seg_here.shape)
    greet(me, plane, rank, planes, HALO)
    for n in range(last):
        for o_at in range(1, PLANE):
            plane_copy(n, o_at).start()
        own_copy(n).start()
    start_chunk(0)
    start_chunk(1)
    own_copy(4).start()
    own_copy(5).start()

    load_o.wait()
    load_g.wait()

    @pl.loop(0, PLANE)
    def _(p):
        sums = []
        for h in range(heads):
            features = pl.ds(pl.multiple_of(p * wide + h * D, D), D)
            product = o_here[:, features].astype(jnp.float32) * g_here[:, features].astype(jnp.float32)
            sums.append(jnp.sum(product.T, axis=0, keepdims=True))
        stats[part(p * 2, heads), :] = lse[part(p, heads), :]
        stats[part(p * 2 + 1, heads), :] = jnp.concatenate(sums, axis=0)

    for o_at in range(1, PLANE):
        plane_copy(last, o_at).start()
    own_copy(last).start()

    for n in range(last):
        own_copy(n).wait()
        for o_at in range(1, PLANE):
            arrival(n, o_at).wait_recv()
        if n == 0:
            for dz in range(1, HALO + 1):
                @pl.when(plane + dz < planes)
                def _():
                    seg_copy(dz).start()
        else:
            @pl.when(plane + 1 < planes)
            def _():
                halo_copy(n - 1, 1).start()
    pass_on(0)
    dk[...] = jnp.zeros_like(dk)
    dv[...] = jnp.zeros_like(dv)
    transpose_keys(0)
    for dz in range(1, HALO + 1):
        @pl.when(plane >= dz)
        def _():
            seg_copy(dz).wait_recv()
    start[...] = begins_at(seg_win[...], own - jnp.minimum(plane, HALO) * span)[:, own:]
    own_copy(last).wait()
    own_copy(4).wait()
    own_copy(5).wait()
    for o_at in range(1, PLANE):
        arrival(last, o_at).wait_recv()

    @pl.loop(0, WHOLE)
    def _(c):
        @pl.when(c + 2 < CHUNKS)
        def _():
            start_chunk(c + 2)

        pass_on(c + 1)
        for path in routes(c):
            path.wait_arrivals()
        for dz in range(HALO + 1):
            if dz > 0:
                @pl.when(c == 0)
                def _():
                    take_halo(dz)

            tiles(c, dz, dz == 0)
        finish_queries(c)
        for n in range(WHOLE):
            @pl.when(c == n)
            def _():
                start_back(n)

    @pl.loop(WHOLE, CHUNKS)
    def _(c):
        @pl.when(c + 1 < CHUNKS)
        def _():
            pass_on(c + 1)

        for path in routes(c):
            path.wait_arrivals()
        tiles(c, 2, True)

    far_out[0] = (dk[:span, :] * inv_root).astype(far_out.dtype)
    far_out[1] = dv[:span, :].astype(far_out.dtype)

    @pl.when(plane >= 2)
    def _():
        for n in range(2):
            far_copy(n).start()

    for n in range(WHOLE):
        back[n].pass_on()

    @pl.loop(WHOLE, CHUNKS)
    def _(c):
        tiles(c, 1, False)

    dk[pl.ds(span, span), :] = dk[pl.ds(span, span), :] * inv_root
    takes_far = (plane >= 1) & (plane + 1 < planes)

    @pl.when(takes_far)
    def _():
        for n in range(2):
            far_copy(n).wait_recv()
            total = (dk, dv)[n]
            near_out[n] = (total[pl.ds(span, span), :] + far_in[n].astype(jnp.float32)).astype(near_out.dtype)

    @pl.when(plane + 1 >= planes)
    def _():
        for n in range(2):
            near_out[n] = (dk, dv)[n][pl.ds(span, span), :].astype(near_out.dtype)

    @pl.when(plane >= 1)
    def _():
        for n in range(2):
            near_copy(n).start()

    for c in range(WHOLE, CHUNKS):
        tiles(c, 0, False)
        finish_queries(c)
        start_back(c)

    dk[pl.ds(own, span), :] = dk[pl.ds(own, span), :] * inv_root
    own_back = pltpu.make_async_copy(dq_low.at[part(rank, rows), :], grad_q.at[:, part(rank, wide)], local.at[4])
    own_back.start()
    back[WHOLE].pass_on()
    own_kv = []
    for n in range(2):
        total = (dk, dv)[n]

        @pl.when(plane + 1 < planes)
        def _():
            near_copy(n).wait_recv()
            low[n] = (total[pl.ds(own, span), :] + near_in[n].astype(jnp.float32)).astype(low.dtype)

        @pl.when(plane + 1 >= planes)
        def _():
            low[n] = total[pl.ds(own, span), :].astype(low.dtype)

        for o_at in range(1, PLANE):
            kv_copy(n, o_at, rank).start()
        own_kv.append(pltpu.make_async_copy(
            low.at[n, part(rank, rows), :], (grad_k, grad_v)[n].at[:, part(rank, D)], local.at[6 + n]
        ))
        own_kv[n].start()
    for c in range(WHOLE + 1, CHUNKS):
        back[c].pass_on()

    own_back.wait()
    for n in range(2):
        own_kv[n].wait()
    for c in range(CHUNKS):
        for path in routes(c):
            path.wait_sends()
        back[c].wait_arrivals()
        back[c].wait_sends()
    for o_at in range(1, PLANE):
        for n in range(last + 1):
            plane_copy(n, o_at).wait_send()
        origin = lax.rem(rank + PLANE - o_at, PLANE)
        for n in range(2):
            kv_copy(n, o_at, origin).wait()
    for dz in range(1, HALO + 1):
        @pl.when(plane + dz < planes)
        def _():
            seg_copy(dz).wait_send()

        @pl.when((plane + 1 < planes) & (plane + 1 >= dz))
        def _():
            for n in range(2):
                halo_copy(n, dz).wait_send()

    @pl.when(plane >= 2)
    def _():
        for n in range(2):
            far_copy(n).wait_send()

    @pl.when(plane >= 1)
    def _():
        for n in range(2):
            near_copy(n).wait_send()


def on_device(q, k, v, o, g, lse, segments):
    planes = lax.axis_size("seq") // PLANE
    rows = q.shape[0]
    span = rows * PLANE
    heads = lse.shape[0] // PLANE
    wide = heads * D
    window = (HALO + 1) * span
    any_space = pl.BlockSpec(memory_space=pl.ANY)
    vmem = pl.BlockSpec(memory_space=pltpu.VMEM)
    low, wider, sems = jnp.bfloat16, jnp.float32, pltpu.SemaphoreType.DMA
    return pl.pallas_call(
        functools.partial(kernel, planes),
        out_shape=(
            jax.ShapeDtypeStruct(q.shape, low),
            jax.ShapeDtypeStruct(k.shape, low),
            jax.ShapeDtypeStruct(v.shape, low),
        ),
        in_specs=[any_space] * 5 + [vmem] * 2,
        out_specs=(any_space,) * 3,
        scratch_shapes=[
            pltpu.VMEM(o.shape, low),
            pltpu.VMEM(g.shape, low),
            pltpu.VMEM((span, wide), low),
            pltpu.VMEM((span, wide), low),
            pltpu.VMEM((window, D), low),
            pltpu.VMEM((window, D), low),
            pltpu.VMEM((D, window), low),
            pltpu.VMEM((8, span), jnp.int32),
            pltpu.VMEM((8, rows), jnp.int32),
            pltpu.VMEM((8, window), jnp.int32),
            pltpu.VMEM((2 * heads * PLANE, rows), wider),
            pltpu.VMEM((2 * heads, span), wider),
            pltpu.VMEM((window, D), wider),
            pltpu.VMEM((window, D), wider),
            pltpu.VMEM((span // BLOCK * D, heads * BLOCK), wider),
            pltpu.VMEM((span, wide), low),
            pltpu.VMEM((2, span, D), low),
            pltpu.VMEM((2, span, D), low),
            pltpu.VMEM((2, span, D), low),
            pltpu.VMEM((2, span, D), low),
            pltpu.VMEM((2, span, D), low),
            pltpu.VMEM((2, CHUNKS, PLANE_X - 1, rows, wide // CHUNKS), low),
            pltpu.VMEM((CHUNKS, PLANE_X - 1, rows, wide // CHUNKS), low),
            sems((2, CHUNKS, ROUTE_SEMS)),
            sems((2, CHUNKS, ROUTE_SEMS)),
            sems((CHUNKS, ROUTE_SEMS)),
            sems((CHUNKS, ROUTE_SEMS)),
            sems((4, PLANE - 1)),
            sems((4, PLANE - 1)),
            sems((2, PLANE - 1)),
            sems((2, PLANE - 1)),
            sems((10,)),
            sems((10,)),
            sems((8,)),
        ],
        compiler_params=pltpu.CompilerParams(
            collective_id=0, has_side_effects=True, vmem_limit_bytes=VMEM_LIMIT
        ),
        name="attention_back",
    )(q, g, o, k, v, segments[None, :], lse)


def solution(mesh):
    rows = P(("dp", "seq"), None)
    in_specs = (rows, rows, rows, rows, rows, P(None, ("dp", "seq")), P(("dp", "seq")))
    return jax.shard_map(
        on_device, mesh=mesh, in_specs=in_specs, out_specs=(rows, rows, rows), check_vma=False
    )
```

```python
import functools
import math

import jax
import jax.numpy as jnp
from jax import lax
from jax.experimental import pallas as pl
from jax.experimental.pallas import tpu as pltpu
from jax.sharding import PartitionSpec as P

D = 128
LOG2E = math.log2(math.e)
MESH = pl.DeviceIdType.MESH
PLANE = 8
PLANE_X = 4
HALO = 2
CHUNKS = 4
WHOLE = 2
ROUTE_SEMS = 10
BLOCK = 256
VMEM_LIMIT = 60 * 1024 * 1024


def dev(index):
    return {"seq": index}


def greet(me, plane, rank, planes, reach):
    barrier = pltpu.get_barrier_semaphore()
    for o in range(1, PLANE):
        peer = plane * PLANE + lax.rem(rank + o, PLANE)
        pl.semaphore_signal(barrier, inc=1, device_id=dev(peer), device_id_type=MESH)
    count = PLANE - 1
    for dz in range(1, reach + 1):
        up = plane + dz < planes
        down = plane >= dz

        @pl.when(up)
        def _():
            pl.semaphore_signal(barrier, inc=1, device_id=dev(me + dz * PLANE), device_id_type=MESH)

        @pl.when(down)
        def _():
            pl.semaphore_signal(barrier, inc=1, device_id=dev(me - dz * PLANE), device_id_type=MESH)

        count = count + up.astype(jnp.int32) + down.astype(jnp.int32)
    pl.semaphore_wait(barrier, count)


class Route:
    def __init__(self, x_first, plane, rank, source, target, stage, sems):
        self.x_first, self.plane = x_first, plane
        self.y, self.x = rank // PLANE_X, lax.rem(rank, PLANE_X)
        self.source, self.target, self.stage = source, target, stage
        self.send, self.recv = sems

    def rank(self, dy, dx):
        y = self.y if dy == 0 else 1 - self.y
        return y * PLANE_X + lax.rem(self.x + dx + PLANE_X, PLANE_X)

    def copy(self, n, source, target, peer):
        return pltpu.make_async_remote_copy(
            source, target, self.send.at[n], self.recv.at[n],
            device_id=dev(self.plane * PLANE + peer), device_id_type=MESH,
        )

    def first_leg(self, dx):
        peer = self.rank(0, dx) if self.x_first else self.rank(1, 0)
        return self.copy(dx - 1, self.source(self.rank(1, dx)), self.stage.at[dx - 1], peer)

    def second_leg(self, dx):
        if self.x_first:
            origin, peer = self.rank(0, -dx), self.rank(1, 0)
        else:
            origin, peer = self.rank(1, 0), self.rank(0, dx)
        return self.copy(2 + dx, self.stage.at[dx - 1], self.target(origin), peer)

    def straight(self, dx):
        peer = self.rank(0, dx) if dx else self.rank(1, 0)
        return self.copy(6 + dx, self.source(peer), self.target(self.rank(0, 0)), peer)

    def start_first(self):
        for dx in range(1, PLANE_X):
            self.first_leg(dx).start()

    def start_straight(self):
        for dx in range(PLANE_X):
            self.straight(dx).start()

    def pass_on(self):
        for dx in range(1, PLANE_X):
            self.first_leg(dx).wait_recv()
            self.second_leg(dx).start()

    def wait_arrivals(self):
        for dx in range(PLANE_X):
            origin = self.rank(0, -dx) if dx else self.rank(1, 0)
            self.copy(6 + dx, self.target(origin), self.target(origin), origin).wait_recv()
        for dx in range(1, PLANE_X):
            origin = self.rank(1, -dx)
            self.copy(2 + dx, self.target(origin), self.target(origin), origin).wait_recv()

    def wait_sends(self):
        for dx in range(1, PLANE_X):
            self.first_leg(dx).wait_send()
            self.second_leg(dx).wait_send()
        for dx in range(PLANE_X):
            self.straight(dx).wait_send()


def tile_terms(k_rows, v_rows, q_rows, g_rows, lse_row, delta_row, visible):
    nt = (((1,), (1,)), ((), ()))
    scores = lax.dot_general(k_rows, q_rows, nt, preferred_element_type=jnp.float32)
    weights = jnp.exp2(scores * (LOG2E / math.sqrt(D)) - lse_row)
    if visible is not None:
        weights = jnp.where(visible(), weights, 0.0)
    d_weights = lax.dot_general(v_rows, g_rows, nt, preferred_element_type=jnp.float32)
    dscore = (weights * (d_weights - delta_row)).astype(jnp.bfloat16)
    return weights.astype(jnp.bfloat16), dscore


def begins_at(ids, first):
    at = lax.broadcasted_iota(jnp.int32, ids.shape, 1)
    begins = (ids != pltpu.roll(ids, 1, 1)) & (at > first)
    found = jnp.where(begins, at, first)
    step = 1
    while step < ids.shape[1]:
        found = jnp.where(at >= step, jnp.maximum(found, pltpu.roll(found, step, 1)), found)
        step *= 2
    return found


def kernel(
    planes, q, g, o, k, v, seg, lse, grad_q, grad_k, grad_v,
    o_here, g_here, q_in, g_in, k_in, v_in, k_t, start, seg_here, seg_win, stats, stats_in,
    dk, dv, dq_t, dq_low, far_out, far_in, near_out, near_in, low, stage, stage_back,
    r_send, r_recv, b_send, b_recv, send, recv, kv_send, kv_recv, z_send, z_recv, local,
):
    rows = q.shape[0]
    span = rows * PLANE
    wide = q_in.shape[1]
    heads = wide // D
    me = lax.axis_index("seq")
    plane, rank = me // PLANE, lax.rem(me, PLANE)
    own = HALO * span
    blocks = span // BLOCK
    narrow = wide // CHUNKS
    per_chunk = narrow // D
    across = per_chunk * BLOCK
    inv_root = 1.0 / math.sqrt(D)

    def part(index, width):
        return pl.ds(pl.multiple_of(index * width, width), width)

    def own_part(s):
        return pl.ds(pl.multiple_of(own + s * rows, rows), rows)

    pieces = [
        (lambda p: seg_here, lambda s: seg_win.at[:, own_part(s)]),
        (lambda p: k.at[:, part(p, D)], lambda s: k_in.at[own_part(s), :]),
        (lambda p: v.at[:, part(p, D)], lambda s: v_in.at[own_part(s), :]),
        (lambda p: stats.at[part(p, 2 * heads), :], lambda s: stats_in.at[:, part(s, rows)]),
        (lambda p: q.at[:, part(p, wide)], lambda s: q_in.at[part(s, rows), :]),
        (lambda p: g.at[:, part(p, wide)], lambda s: g_in.at[part(s, rows), :]),
    ]
    last = 3

    def routes(c):
        made = []
        for n, (array, gathered) in enumerate(((q, q_in), (g, g_in))):
            def source(p, array=array):
                return array.at[:, pl.ds(pl.multiple_of(p * wide + c * narrow, narrow), narrow)]

            def target(s, gathered=gathered):
                return gathered.at[part(s, rows), part(c, narrow)]

            made.append(Route(
                n == 0, plane, rank, source, target, stage.at[n, c], (r_send.at[n, c], r_recv.at[n, c])
            ))
        return made

    def route_back(c):
        def source(p):
            return dq_low.at[part(p, rows), pl.ds(c * narrow, narrow)]

        def target(s):
            return grad_q.at[:, pl.ds(pl.multiple_of(s * wide + c * narrow, narrow), narrow)]

        return Route(c % 2 == 0, plane, rank, source, target, stage_back.at[c], (b_send.at[c], b_recv.at[c]))

    back = [route_back(c) for c in range(CHUNKS)]

    def own_copy(n):
        source, target = pieces[n]
        return pltpu.make_async_copy(source(rank), target(rank), local.at[n])

    def plane_copy(n, o):
        source, target = pieces[n]
        peer = lax.rem(rank + o, PLANE)
        return pltpu.make_async_remote_copy(
            source(peer), target(rank), send.at[n, o - 1], recv.at[n, o - 1],
            device_id=dev(plane * PLANE + peer), device_id_type=MESH,
        )

    def arrival(n, o):
        source, target = pieces[n]
        origin = lax.rem(rank + PLANE - o, PLANE)
        return pltpu.make_async_remote_copy(
            source(rank), target(origin), send.at[n, o - 1], recv.at[n, o - 1],
            device_id=dev(plane * PLANE + origin), device_id_type=MESH,
        )

    def kv_copy(n, o, origin):
        peer = lax.rem(rank + o, PLANE)
        return pltpu.make_async_remote_copy(
            low.at[n, part(peer, rows), :], (grad_k, grad_v)[n].at[:, part(origin, D)],
            kv_send.at[n, o - 1], kv_recv.at[n, o - 1],
            device_id=dev(plane * PLANE + peer), device_id_type=MESH,
        )

    def z_copy(n, source, target, planes_on):
        return pltpu.make_async_remote_copy(
            source, target, z_send.at[n], z_recv.at[n],
            device_id=dev(me + planes_on * PLANE), device_id_type=MESH,
        )

    def seg_copy(dz):
        return z_copy(dz - 1, seg_win.at[:, pl.ds(own, span)], seg_win.at[:, pl.ds(own - dz * span, span)], dz)

    def halo_copy(n, dz):
        win = (k_in, v_in)[n]
        held, there = pl.ds(own - (dz - 1) * span, span), pl.ds(own - dz * span, span)
        return z_copy(2 * dz + n, win.at[held, :], win.at[there, :], 1)

    def far_copy(n):
        return z_copy(6 + n, far_out.at[n], far_in.at[n], -1)

    def near_copy(n):
        return z_copy(8 + n, near_out.at[n], near_in.at[n], -1)

    def start_chunk(c):
        for path in routes(c):
            path.start_first()
        for path in routes(c):
            path.start_straight()

    def pass_on(c):
        for path in routes(c):
            path.pass_on()

    def start_back(c):
        back[c].start_first()
        back[c].start_straight()

    def transpose_keys(dz):
        held = pl.ds(own - dz * span, span)
        k_t[:, held] = k_in[held, :].T

    def take_halo(dz):
        held = pl.ds(own - dz * span, span)

        @pl.when(plane >= dz)
        def _():
            for n in range(2):
                halo_copy(n, dz).wait_recv()

        @pl.when(plane < dz)
        def _():
            k_in[held, :] = jnp.zeros((span, D), k_in.dtype)
            v_in[held, :] = jnp.zeros((span, D), v_in.dtype)

        if dz < HALO:
            @pl.when((plane >= dz) & (plane + 1 < planes))
            def _():
                for n in range(2):
                    halo_copy(n, dz + 1).start()
        transpose_keys(dz)

    def tiles(c, dz, first):
        operands = []
        for i in range(blocks):
            here = pl.ds(i * BLOCK, BLOCK)

            def stacked(ref, here=here):
                return jnp.concatenate(
                    [ref[here, pl.ds(pl.multiple_of(c * narrow + h * D, D), D)] for h in range(per_chunk)], axis=0
                )

            def in_line(at, here=here):
                return jnp.concatenate(
                    [stats_in[pl.ds(at + c * per_chunk + h, 1), here] for h in range(per_chunk)], axis=1
                )

            start_row = jnp.concatenate([start[0:1, here]] * per_chunk, axis=1)
            operands.append((stacked(q_in), stacked(g_in), in_line(0) * LOG2E, in_line(heads), start_row))
        totals = [None] * blocks
        down = lax.broadcasted_iota(jnp.int32, (BLOCK, across), 0)
        query_at = lax.rem(lax.broadcasted_iota(jnp.int32, (1, across), 1), BLOCK)
        for before in range(HALO * blocks + 1):
            for i in range(blocks):
                j = HALO * blocks + i - before
                if j // blocks != HALO - dz:
                    continue
                there = pl.ds(j * BLOCK, BLOCK)
                q_rows, g_rows, lse_row, delta_row, start_row = operands[i]

                def visible(j=j, before=before, start_row=start_row):
                    seen = down >= start_row - j * BLOCK
                    return seen & (down <= query_at) if before == 0 else seen

                weights, dscore = tile_terms(
                    k_in[there, :], v_in[there, :], q_rows, g_rows, lse_row, delta_row, visible
                )
                dv[there, :] += jnp.dot(weights, g_rows, preferred_element_type=jnp.float32)
                dk[there, :] += jnp.dot(dscore, q_rows, preferred_element_type=jnp.float32)
                term = jnp.dot(k_t[:, there], dscore, preferred_element_type=jnp.float32)
                totals[i] = term if totals[i] is None else totals[i] + term
        for i in range(blocks):
            if first:
                dq_t[pl.ds(i * D, D), part(c, across)] = totals[i]
            else:
                dq_t[pl.ds(i * D, D), part(c, across)] += totals[i]

    def finish_queries(c):
        for i in range(blocks):
            for h in range(per_chunk):
                total = dq_t[pl.ds(i * D, D), pl.ds(pl.multiple_of(c * across + h * BLOCK, BLOCK), BLOCK)]
                dq_low[pl.ds(i * BLOCK, BLOCK), pl.ds(pl.multiple_of(c * narrow + h * D, D), D)] = (
                    total.T * inv_root
                ).astype(dq_low.dtype)

    load_o = pltpu.make_async_copy(o, o_here, local.at[6])
    load_g = pltpu.make_async_copy(g, g_here, local.at[7])
    load_o.start()
    load_g.start()
    seg_here[...] = jnp.broadcast_to(seg[...], seg_here.shape)
    greet(me, plane, rank, planes, HALO)
    for n in range(last):
        for o_at in range(1, PLANE):
            plane_copy(n, o_at).start()
        own_copy(n).start()
    start_chunk(0)
    own_copy(4).start()
    own_copy(5).start()
    for n in range(last):
        own_copy(n).wait()
        for o_at in range(1, PLANE):
            arrival(n, o_at).wait_recv()
        if n == 0:
            for dz in range(1, HALO + 1):
                @pl.when(plane + dz < planes)
                def _():
                    seg_copy(dz).start()
        else:
            @pl.when(plane + 1 < planes)
            def _():
                halo_copy(n - 1, 1).start()
    pass_on(0)

    load_o.wait()
    load_g.wait()

    @pl.loop(0, PLANE)
    def _(p):
        sums = []
        for h in range(heads):
            features = pl.ds(pl.multiple_of(p * wide + h * D, D), D)
            product = o_here[:, features].astype(jnp.float32) * g_here[:, features].astype(jnp.float32)
            sums.append(jnp.sum(product.T, axis=0, keepdims=True))
        stats[part(p * 2, heads), :] = lse[part(p, heads), :]
        stats[part(p * 2 + 1, heads), :] = jnp.concatenate(sums, axis=0)

    for o_at in range(1, PLANE):
        plane_copy(last, o_at).start()
    own_copy(last).start()
    start_chunk(1)
    dk[...] = jnp.zeros_like(dk)
    dv[...] = jnp.zeros_like(dv)
    transpose_keys(0)
    for dz in range(1, HALO + 1):
        @pl.when(plane >= dz)
        def _():
            seg_copy(dz).wait_recv()
    start[...] = begins_at(seg_win[...], own - jnp.minimum(plane, HALO) * span)[:, own:]
    own_copy(last).wait()
    own_copy(4).wait()
    own_copy(5).wait()
    for o_at in range(1, PLANE):
        arrival(last, o_at).wait_recv()

    @pl.loop(0, WHOLE)
    def _(c):
        for path in routes(c):
            path.wait_arrivals()
        for dz in range(HALO + 1):
            if dz > 0:
                @pl.when(c == 0)
                def _():
                    take_halo(dz)

            tiles(c, dz, dz == 0)
            if dz == 0:
                pass_on(c + 1)
                start_chunk(c + 2)
            if dz == 1:
                @pl.when(c == WHOLE - 1)
                def _():
                    pass_on(WHOLE + 1)
                    back[0].pass_on()

        finish_queries(c)
        for n in range(WHOLE):
            @pl.when(c == n)
            def _():
                start_back(n)

    @pl.loop(WHOLE, CHUNKS)
    def _(c):
        for path in routes(c):
            path.wait_arrivals()
        tiles(c, 2, True)

    far_out[0] = (dk[:span, :] * inv_root).astype(far_out.dtype)
    far_out[1] = dv[:span, :].astype(far_out.dtype)

    @pl.when(plane >= 2)
    def _():
        for n in range(2):
            far_copy(n).start()

    back[1].pass_on()

    @pl.loop(WHOLE, CHUNKS)
    def _(c):
        tiles(c, 1, False)

    dk[pl.ds(span, span), :] = dk[pl.ds(span, span), :] * inv_root
    takes_far = (plane >= 1) & (plane + 1 < planes)

    @pl.when(takes_far)
    def _():
        for n in range(2):
            far_copy(n).wait_recv()
            total = (dk, dv)[n]
            near_out[n] = (total[pl.ds(span, span), :] + far_in[n].astype(jnp.float32)).astype(near_out.dtype)

    @pl.when(plane + 1 >= planes)
    def _():
        for n in range(2):
            near_out[n] = (dk, dv)[n][pl.ds(span, span), :].astype(near_out.dtype)

    @pl.when(plane >= 1)
    def _():
        for n in range(2):
            near_copy(n).start()

    for c in range(WHOLE, CHUNKS):
        tiles(c, 0, False)
        finish_queries(c)
        start_back(c)

    dk[pl.ds(own, span), :] = dk[pl.ds(own, span), :] * inv_root
    own_back = pltpu.make_async_copy(dq_low.at[part(rank, rows), :], grad_q.at[:, part(rank, wide)], local.at[4])
    own_back.start()
    back[WHOLE].pass_on()
    own_kv = []
    for n in range(2):
        total = (dk, dv)[n]

        @pl.when(plane + 1 < planes)
        def _():
            near_copy(n).wait_recv()
            low[n] = (total[pl.ds(own, span), :] + near_in[n].astype(jnp.float32)).astype(low.dtype)

        @pl.when(plane + 1 >= planes)
        def _():
            low[n] = total[pl.ds(own, span), :].astype(low.dtype)

        for o_at in range(1, PLANE):
            kv_copy(n, o_at, rank).start()
        own_kv.append(pltpu.make_async_copy(
            low.at[n, part(rank, rows), :], (grad_k, grad_v)[n].at[:, part(rank, D)], local.at[6 + n]
        ))
        own_kv[n].start()
    for c in range(WHOLE + 1, CHUNKS):
        back[c].pass_on()

    own_back.wait()
    for n in range(2):
        own_kv[n].wait()
    for c in range(CHUNKS):
        for path in routes(c):
            path.wait_sends()
        back[c].wait_arrivals()
        back[c].wait_sends()
    for o_at in range(1, PLANE):
        for n in range(last + 1):
            plane_copy(n, o_at).wait_send()
        origin = lax.rem(rank + PLANE - o_at, PLANE)
        for n in range(2):
            kv_copy(n, o_at, origin).wait()
    for dz in range(1, HALO + 1):
        @pl.when(plane + dz < planes)
        def _():
            seg_copy(dz).wait_send()

        @pl.when((plane + 1 < planes) & (plane + 1 >= dz))
        def _():
            for n in range(2):
                halo_copy(n, dz).wait_send()

    @pl.when(plane >= 2)
    def _():
        for n in range(2):
            far_copy(n).wait_send()

    @pl.when(plane >= 1)
    def _():
        for n in range(2):
            near_copy(n).wait_send()


def hand_over(*refs):
    for source, target in zip(refs[:3], refs[3:]):
        target[...] = source[...]


def on_device(q, k, v, o, g, lse, segments):
    planes = lax.axis_size("seq") // PLANE
    rows = q.shape[0]
    span = rows * PLANE
    heads = lse.shape[0] // PLANE
    wide = heads * D
    window = (HALO + 1) * span
    any_space = pl.BlockSpec(memory_space=pl.ANY)
    vmem = pl.BlockSpec(memory_space=pltpu.VMEM)
    low, wider, sems = jnp.bfloat16, jnp.float32, pltpu.SemaphoreType.DMA
    grads = pl.pallas_call(
        functools.partial(kernel, planes),
        out_shape=(
            jax.ShapeDtypeStruct(q.shape, low),
            jax.ShapeDtypeStruct(k.shape, low),
            jax.ShapeDtypeStruct(v.shape, low),
        ),
        in_specs=[any_space] * 5 + [vmem] * 2,
        out_specs=(any_space,) * 3,
        scratch_shapes=[
            pltpu.VMEM(o.shape, low),
            pltpu.VMEM(g.shape, low),
            pltpu.VMEM((span, wide), low),
            pltpu.VMEM((span, wide), low),
            pltpu.VMEM((window, D), low),
            pltpu.VMEM((window, D), low),
            pltpu.VMEM((D, window), low),
            pltpu.VMEM((8, span), jnp.int32),
            pltpu.VMEM((8, rows), jnp.int32),
            pltpu.VMEM((8, window), jnp.int32),
            pltpu.VMEM((2 * heads * PLANE, rows), wider),
            pltpu.VMEM((2 * heads, span), wider),
            pltpu.VMEM((window, D), wider),
            pltpu.VMEM((window, D), wider),
            pltpu.VMEM((span // BLOCK * D, heads * BLOCK), wider),
            pltpu.VMEM((span, wide), low),
            pltpu.VMEM((2, span, D), low),
            pltpu.VMEM((2, span, D), low),
            pltpu.VMEM((2, span, D), low),
            pltpu.VMEM((2, span, D), low),
            pltpu.VMEM((2, span, D), low),
            pltpu.VMEM((2, CHUNKS, PLANE_X - 1, rows, wide // CHUNKS), low),
            pltpu.VMEM((CHUNKS, PLANE_X - 1, rows, wide // CHUNKS), low),
            sems((2, CHUNKS, ROUTE_SEMS)),
            sems((2, CHUNKS, ROUTE_SEMS)),
            sems((CHUNKS, ROUTE_SEMS)),
            sems((CHUNKS, ROUTE_SEMS)),
            sems((4, PLANE - 1)),
            sems((4, PLANE - 1)),
            sems((2, PLANE - 1)),
            sems((2, PLANE - 1)),
            sems((10,)),
            sems((10,)),
            sems((8,)),
        ],
        compiler_params=pltpu.CompilerParams(
            collective_id=0, has_side_effects=True, vmem_limit_bytes=VMEM_LIMIT
        ),
        name="attention_back",
    )(q, g, o, k, v, segments[None, :], lse)
    cut = [pl.BlockSpec((rows // 4, x.shape[1]), lambda i: (i, 0)) for x in grads]
    return pl.pallas_call(
        hand_over,
        grid=(4,),
        in_specs=cut,
        out_specs=cut,
        out_shape=[jax.ShapeDtypeStruct(x.shape, x.dtype) for x in grads],
        compiler_params=pltpu.CompilerParams(vmem_limit_bytes=VMEM_LIMIT),
        name="hand_over",
    )(*grads)


def solution(mesh):
    rows = P(("dp", "seq"), None)
    in_specs = (rows, rows, rows, rows, rows, P(None, ("dp", "seq")), P(("dp", "seq")))
    return jax.shard_map(
        on_device, mesh=mesh, in_specs=in_specs, out_specs=(rows, rows, rows), check_vma=False
    )
```

```python
import functools
import math

import jax
import jax.numpy as jnp
from jax import lax
from jax.experimental import pallas as pl
from jax.experimental.pallas import tpu as pltpu
from jax.sharding import PartitionSpec as P

D = 128
LOG2E = math.log2(math.e)
MESH = pl.DeviceIdType.MESH
PLANE = 8
PLANE_X = 4
HALO = 2
CHUNKS = 4
PIECES = 4
WHOLE = 2
ROUTE_SEMS = 10
BLOCK = 256
VMEM_LIMIT = 60 * 1024 * 1024


def dev(index):
    return {"seq": index}


def greet(me, plane, rank, planes, reach):
    barrier = pltpu.get_barrier_semaphore()
    for o in range(1, PLANE):
        peer = plane * PLANE + lax.rem(rank + o, PLANE)
        pl.semaphore_signal(barrier, inc=1, device_id=dev(peer), device_id_type=MESH)
    count = PLANE - 1
    for dz in range(1, reach + 1):
        up = plane + dz < planes
        down = plane >= dz

        @pl.when(up)
        def _():
            pl.semaphore_signal(barrier, inc=1, device_id=dev(me + dz * PLANE), device_id_type=MESH)

        @pl.when(down)
        def _():
            pl.semaphore_signal(barrier, inc=1, device_id=dev(me - dz * PLANE), device_id_type=MESH)

        count = count + up.astype(jnp.int32) + down.astype(jnp.int32)
    pl.semaphore_wait(barrier, count)


class Route:
    def __init__(self, x_first, plane, rank, source, target, stage, sems):
        self.x_first, self.plane = x_first, plane
        self.y, self.x = rank // PLANE_X, lax.rem(rank, PLANE_X)
        self.source, self.target, self.stage = source, target, stage
        self.send, self.recv = sems

    def rank(self, dy, dx):
        y = self.y if dy == 0 else 1 - self.y
        return y * PLANE_X + lax.rem(self.x + dx + PLANE_X, PLANE_X)

    def copy(self, n, source, target, peer):
        return pltpu.make_async_remote_copy(
            source, target, self.send.at[n], self.recv.at[n],
            device_id=dev(self.plane * PLANE + peer), device_id_type=MESH,
        )

    def first_leg(self, dx):
        peer = self.rank(0, dx) if self.x_first else self.rank(1, 0)
        return self.copy(dx - 1, self.source(self.rank(1, dx)), self.stage.at[dx - 1], peer)

    def second_leg(self, dx):
        if self.x_first:
            origin, peer = self.rank(0, -dx), self.rank(1, 0)
        else:
            origin, peer = self.rank(1, 0), self.rank(0, dx)
        return self.copy(2 + dx, self.stage.at[dx - 1], self.target(origin), peer)

    def straight(self, dx):
        peer = self.rank(0, dx) if dx else self.rank(1, 0)
        return self.copy(6 + dx, self.source(peer), self.target(self.rank(0, 0)), peer)

    def start_first(self):
        for dx in range(1, PLANE_X):
            self.first_leg(dx).start()

    def start_straight(self):
        for dx in range(PLANE_X):
            self.straight(dx).start()

    def pass_on(self):
        for dx in range(1, PLANE_X):
            self.first_leg(dx).wait_recv()
            self.second_leg(dx).start()

    def wait_arrivals(self):
        for dx in range(PLANE_X):
            origin = self.rank(0, -dx) if dx else self.rank(1, 0)
            self.copy(6 + dx, self.target(origin), self.target(origin), origin).wait_recv()
        for dx in range(1, PLANE_X):
            origin = self.rank(1, -dx)
            self.copy(2 + dx, self.target(origin), self.target(origin), origin).wait_recv()

    def wait_sends(self):
        for dx in range(1, PLANE_X):
            self.first_leg(dx).wait_send()
            self.second_leg(dx).wait_send()
        for dx in range(PLANE_X):
            self.straight(dx).wait_send()


def tile_terms(k_rows, v_rows, q_rows, g_rows, lse_row, delta_row, visible):
    nt = (((1,), (1,)), ((), ()))
    scores = lax.dot_general(k_rows, q_rows, nt, preferred_element_type=jnp.float32)
    weights = jnp.exp2(scores * (LOG2E / math.sqrt(D)) - lse_row)
    if visible is not None:
        weights = jnp.where(visible(), weights, 0.0)
    d_weights = lax.dot_general(v_rows, g_rows, nt, preferred_element_type=jnp.float32)
    dscore = (weights * (d_weights - delta_row)).astype(jnp.bfloat16)
    return weights.astype(jnp.bfloat16), dscore


def begins_at(ids, first):
    at = lax.broadcasted_iota(jnp.int32, ids.shape, 1)
    begins = (ids != pltpu.roll(ids, 1, 1)) & (at > first)
    found = jnp.where(begins, at, first)
    step = 1
    while step < ids.shape[1]:
        found = jnp.where(at >= step, jnp.maximum(found, pltpu.roll(found, step, 1)), found)
        step *= 2
    return found


def kernel(
    planes, q, g, o, k, v, seg, lse, grad_q, grad_k, grad_v,
    o_here, g_here, q_in, g_in, k_in, v_in, k_t, start, seg_here, seg_win, stats, stats_in,
    dk, dv, dq_t, dq_low, far_out, far_in, near_out, near_in, low, stage, stage_back,
    r_send, r_recv, b_send, b_recv, send, recv, kv_send, kv_recv, z_send, z_recv, local,
):
    rows = q.shape[0]
    span = rows * PLANE
    wide = q_in.shape[1]
    heads = wide // D
    me = lax.axis_index("seq")
    plane, rank = me // PLANE, lax.rem(me, PLANE)
    own = HALO * span
    blocks = span // BLOCK
    narrow = wide // CHUNKS
    per_chunk = narrow // D
    across = per_chunk * BLOCK
    inv_root = 1.0 / math.sqrt(D)

    def part(index, width):
        return pl.ds(pl.multiple_of(index * width, width), width)

    def own_part(s):
        return pl.ds(pl.multiple_of(own + s * rows, rows), rows)

    pieces = [
        (lambda p: seg_here, lambda s: seg_win.at[:, own_part(s)]),
        (lambda p: k.at[:, part(p, D)], lambda s: k_in.at[own_part(s), :]),
        (lambda p: v.at[:, part(p, D)], lambda s: v_in.at[own_part(s), :]),
        (lambda p: stats.at[part(p, 2 * heads), :], lambda s: stats_in.at[:, part(s, rows)]),
        (lambda p: q.at[:, part(p, wide)], lambda s: q_in.at[part(s, rows), :]),
        (lambda p: g.at[:, part(p, wide)], lambda s: g_in.at[part(s, rows), :]),
    ]
    last = 3

    def routes(c):
        made = []
        for n, (array, gathered) in enumerate(((q, q_in), (g, g_in))):
            def source(p, array=array):
                return array.at[:, pl.ds(pl.multiple_of(p * wide + c * narrow, narrow), narrow)]

            def target(s, gathered=gathered):
                return gathered.at[part(s, rows), part(c, narrow)]

            made.append(Route(
                n == 0, plane, rank, source, target, stage.at[n, c], (r_send.at[n, c], r_recv.at[n, c])
            ))
        return made

    def route_back(c):
        def source(p):
            return dq_low.at[part(p, rows), pl.ds(c * narrow, narrow)]

        def target(s):
            return grad_q.at[:, pl.ds(pl.multiple_of(s * wide + c * narrow, narrow), narrow)]

        return Route(c % 2 == 0, plane, rank, source, target, stage_back.at[c], (b_send.at[c], b_recv.at[c]))

    back = [route_back(c) for c in range(CHUNKS)]

    def own_copy(n):
        source, target = pieces[n]
        return pltpu.make_async_copy(source(rank), target(rank), local.at[n])

    def plane_copy(n, o):
        source, target = pieces[n]
        peer = lax.rem(rank + o, PLANE)
        return pltpu.make_async_remote_copy(
            source(peer), target(rank), send.at[n, o - 1], recv.at[n, o - 1],
            device_id=dev(plane * PLANE + peer), device_id_type=MESH,
        )

    def arrival(n, o):
        source, target = pieces[n]
        origin = lax.rem(rank + PLANE - o, PLANE)
        return pltpu.make_async_remote_copy(
            source(rank), target(origin), send.at[n, o - 1], recv.at[n, o - 1],
            device_id=dev(plane * PLANE + origin), device_id_type=MESH,
        )

    def kv_copy(n, o, origin):
        peer = lax.rem(rank + o, PLANE)
        return pltpu.make_async_remote_copy(
            low.at[n, part(peer, rows), :], (grad_k, grad_v)[n].at[:, part(origin, D)],
            kv_send.at[n, o - 1], kv_recv.at[n, o - 1],
            device_id=dev(plane * PLANE + peer), device_id_type=MESH,
        )

    def z_copy(n, source, target, planes_on):
        return pltpu.make_async_remote_copy(
            source, target, z_send.at[n], z_recv.at[n],
            device_id=dev(me + planes_on * PLANE), device_id_type=MESH,
        )

    def seg_copy(dz):
        return z_copy(dz - 1, seg_win.at[:, pl.ds(own, span)], seg_win.at[:, pl.ds(own - dz * span, span)], dz)

    def halo_copy(n, dz):
        win = (k_in, v_in)[n]
        held, there = pl.ds(own - (dz - 1) * span, span), pl.ds(own - dz * span, span)
        return z_copy(2 * dz + n, win.at[held, :], win.at[there, :], 1)

    def far_copy(n):
        return z_copy(6 + n, far_out.at[n], far_in.at[n], -1)

    def near_copy(n):
        return z_copy(8 + n, near_out.at[n], near_in.at[n], -1)

    def start_chunk(c):
        for path in routes(c):
            path.start_first()
        for path in routes(c):
            path.start_straight()

    def pass_on(c):
        for path in routes(c):
            path.pass_on()

    def start_back(c):
        back[c].start_first()
        back[c].start_straight()

    def transpose_keys(dz):
        held = pl.ds(own - dz * span, span)
        k_t[:, held] = k_in[held, :].T

    def take_halo(dz):
        held = pl.ds(own - dz * span, span)

        @pl.when(plane >= dz)
        def _():
            for n in range(2):
                halo_copy(n, dz).wait_recv()

        @pl.when(plane < dz)
        def _():
            k_in[held, :] = jnp.zeros((span, D), k_in.dtype)
            v_in[held, :] = jnp.zeros((span, D), v_in.dtype)

        if dz < HALO:
            @pl.when((plane >= dz) & (plane + 1 < planes))
            def _():
                for n in range(2):
                    halo_copy(n, dz + 1).start()
        transpose_keys(dz)

    def tiles(c, dz, first):
        operands = []
        for i in range(blocks):
            here = pl.ds(i * BLOCK, BLOCK)

            def stacked(ref, here=here):
                return jnp.concatenate(
                    [ref[here, pl.ds(pl.multiple_of(c * narrow + h * D, D), D)] for h in range(per_chunk)], axis=0
                )

            def in_line(at, here=here):
                return jnp.concatenate(
                    [stats_in[pl.ds(at + c * per_chunk + h, 1), here] for h in range(per_chunk)], axis=1
                )

            start_row = jnp.concatenate([start[0:1, here]] * per_chunk, axis=1)
            operands.append((stacked(q_in), stacked(g_in), in_line(0) * LOG2E, in_line(heads), start_row))
        totals = [None] * blocks
        down = lax.broadcasted_iota(jnp.int32, (BLOCK, across), 0)
        query_at = lax.rem(lax.broadcasted_iota(jnp.int32, (1, across), 1), BLOCK)
        for before in range(HALO * blocks + 1):
            for i in range(blocks):
                j = HALO * blocks + i - before
                if j // blocks != HALO - dz:
                    continue
                there = pl.ds(j * BLOCK, BLOCK)
                q_rows, g_rows, lse_row, delta_row, start_row = operands[i]

                def visible(j=j, before=before, start_row=start_row):
                    seen = down >= start_row - j * BLOCK
                    return seen & (down <= query_at) if before == 0 else seen

                weights, dscore = tile_terms(
                    k_in[there, :], v_in[there, :], q_rows, g_rows, lse_row, delta_row, visible
                )
                dv[there, :] += jnp.dot(weights, g_rows, preferred_element_type=jnp.float32)
                dk[there, :] += jnp.dot(dscore, q_rows, preferred_element_type=jnp.float32)
                term = jnp.dot(k_t[:, there], dscore, preferred_element_type=jnp.float32)
                totals[i] = term if totals[i] is None else totals[i] + term
        for i in range(blocks):
            if first:
                dq_t[pl.ds(i * D, D), part(c, across)] = totals[i]
            else:
                dq_t[pl.ds(i * D, D), part(c, across)] += totals[i]

    def finish_queries(c):
        for i in range(blocks):
            for h in range(per_chunk):
                total = dq_t[pl.ds(i * D, D), pl.ds(pl.multiple_of(c * across + h * BLOCK, BLOCK), BLOCK)]
                dq_low[pl.ds(i * BLOCK, BLOCK), pl.ds(pl.multiple_of(c * narrow + h * D, D), D)] = (
                    total.T * inv_root
                ).astype(dq_low.dtype)

    load_o = pltpu.make_async_copy(o, o_here, local.at[6])
    load_g = pltpu.make_async_copy(g, g_here, local.at[7])
    load_o.start()
    load_g.start()
    seg_here[...] = jnp.broadcast_to(seg[...], seg_here.shape)
    greet(me, plane, rank, planes, HALO)
    for n in range(last):
        if n == 1:
            for path in routes(0):
                path.start_first()
        for o_at in range(1, PLANE):
            plane_copy(n, o_at).start()
        own_copy(n).start()
    for path in routes(0):
        path.start_straight()
    own_copy(4).start()
    own_copy(5).start()
    for n in range(last):
        own_copy(n).wait()
        for o_at in range(1, PLANE):
            arrival(n, o_at).wait_recv()
        if n == 0:
            for dz in range(1, HALO + 1):
                @pl.when(plane + dz < planes)
                def _():
                    seg_copy(dz).start()
            pass_on(0)
        else:
            @pl.when(plane + 1 < planes)
            def _():
                halo_copy(n - 1, 1).start()

    load_o.wait()
    load_g.wait()

    @pl.loop(0, PLANE)
    def _(p):
        sums = []
        for h in range(heads):
            features = pl.ds(pl.multiple_of(p * wide + h * D, D), D)
            product = o_here[:, features].astype(jnp.float32) * g_here[:, features].astype(jnp.float32)
            sums.append(jnp.sum(product.T, axis=0, keepdims=True))
        stats[part(p * 2, heads), :] = lse[part(p, heads), :]
        stats[part(p * 2 + 1, heads), :] = jnp.concatenate(sums, axis=0)

    for o_at in range(1, PLANE):
        plane_copy(last, o_at).start()
    own_copy(last).start()
    start_chunk(1)
    dk[...] = jnp.zeros_like(dk)
    dv[...] = jnp.zeros_like(dv)
    transpose_keys(0)
    for dz in range(1, HALO + 1):
        @pl.when(plane >= dz)
        def _():
            seg_copy(dz).wait_recv()
    start[...] = begins_at(seg_win[...], own - jnp.minimum(plane, HALO) * span)[:, own:]
    own_copy(last).wait()
    own_copy(4).wait()
    own_copy(5).wait()
    for o_at in range(1, PLANE):
        arrival(last, o_at).wait_recv()

    @pl.loop(0, WHOLE)
    def _(c):
        for path in routes(c):
            path.wait_arrivals()
        for dz in range(HALO + 1):
            if dz > 0:
                @pl.when(c == 0)
                def _():
                    take_halo(dz)

            tiles(c, dz, dz == 0)
            if dz == 0:
                pass_on(c + 1)
                start_chunk(c + 2)
            if dz == 1:
                @pl.when(c == WHOLE - 1)
                def _():
                    pass_on(WHOLE + 1)
                    back[0].pass_on()

        finish_queries(c)
        for n in range(WHOLE):
            @pl.when(c == n)
            def _():
                start_back(n)

    @pl.loop(WHOLE, CHUNKS)
    def _(c):
        for path in routes(c):
            path.wait_arrivals()
        tiles(c, 2, True)

    far_out[0] = (dk[:span, :] * inv_root).astype(far_out.dtype)
    far_out[1] = dv[:span, :].astype(far_out.dtype)

    @pl.when(plane >= 2)
    def _():
        for n in range(2):
            far_copy(n).start()

    back[1].pass_on()

    @pl.loop(WHOLE, CHUNKS)
    def _(c):
        tiles(c, 1, False)

    dk[pl.ds(span, span), :] = dk[pl.ds(span, span), :] * inv_root
    takes_far = (plane >= 1) & (plane + 1 < planes)

    @pl.when(takes_far)
    def _():
        for n in range(2):
            far_copy(n).wait_recv()
            total = (dk, dv)[n]
            near_out[n] = (total[pl.ds(span, span), :] + far_in[n].astype(jnp.float32)).astype(near_out.dtype)

    @pl.when(plane + 1 >= planes)
    def _():
        for n in range(2):
            near_out[n] = (dk, dv)[n][pl.ds(span, span), :].astype(near_out.dtype)

    @pl.when(plane >= 1)
    def _():
        for n in range(2):
            near_copy(n).start()

    for c in range(WHOLE, CHUNKS):
        tiles(c, 0, False)
        finish_queries(c)
        start_back(c)

    dk[pl.ds(own, span), :] = dk[pl.ds(own, span), :] * inv_root
    own_back = pltpu.make_async_copy(dq_low.at[part(rank, rows), :], grad_q.at[:, part(rank, wide)], local.at[4])
    own_back.start()
    back[WHOLE].pass_on()
    own_kv = []
    for n in range(2):
        total = (dk, dv)[n]

        @pl.when(plane + 1 < planes)
        def _():
            near_copy(n).wait_recv()
            low[n] = (total[pl.ds(own, span), :] + near_in[n].astype(jnp.float32)).astype(low.dtype)

        @pl.when(plane + 1 >= planes)
        def _():
            low[n] = total[pl.ds(own, span), :].astype(low.dtype)

        for o_at in range(1, PLANE):
            kv_copy(n, o_at, rank).start()
        own_kv.append(pltpu.make_async_copy(
            low.at[n, part(rank, rows), :], (grad_k, grad_v)[n].at[:, part(rank, D)], local.at[6 + n]
        ))
        own_kv[n].start()
    for c in range(WHOLE + 1, CHUNKS):
        back[c].pass_on()

    own_back.wait()
    for n in range(2):
        own_kv[n].wait()
    for c in range(CHUNKS):
        for path in routes(c):
            path.wait_sends()
        back[c].wait_arrivals()
        back[c].wait_sends()
    for o_at in range(1, PLANE):
        for n in range(last + 1):
            plane_copy(n, o_at).wait_send()
        origin = lax.rem(rank + PLANE - o_at, PLANE)
        for n in range(2):
            kv_copy(n, o_at, origin).wait()
    for dz in range(1, HALO + 1):
        @pl.when(plane + dz < planes)
        def _():
            seg_copy(dz).wait_send()

        @pl.when((plane + 1 < planes) & (plane + 1 >= dz))
        def _():
            for n in range(2):
                halo_copy(n, dz).wait_send()

    @pl.when(plane >= 2)
    def _():
        for n in range(2):
            far_copy(n).wait_send()

    @pl.when(plane >= 1)
    def _():
        for n in range(2):
            near_copy(n).wait_send()


def hand_over(*refs):
    sources, targets, held, arrived, left = refs[:3], refs[3:6], refs[6:9], refs[9], refs[10]
    copies = []
    for n in range(3):
        rows = sources[n].shape[0] // PIECES
        for m in range(PIECES):
            at = pl.ds(m * rows, rows)
            copies.append((
                pltpu.make_async_copy(sources[n].at[at, :], held[n].at[at, :], arrived.at[n, m]),
                pltpu.make_async_copy(held[n].at[at, :], targets[n].at[at, :], left.at[n, m]),
            ))
    for load, _ in copies:
        load.start()
    for load, store in copies:
        load.wait()
        store.start()
    for _, store in copies:
        store.wait()


def on_device(q, k, v, o, g, lse, segments):
    planes = lax.axis_size("seq") // PLANE
    rows = q.shape[0]
    span = rows * PLANE
    heads = lse.shape[0] // PLANE
    wide = heads * D
    window = (HALO + 1) * span
    any_space = pl.BlockSpec(memory_space=pl.ANY)
    vmem = pl.BlockSpec(memory_space=pltpu.VMEM)
    low, wider, sems = jnp.bfloat16, jnp.float32, pltpu.SemaphoreType.DMA
    grads = pl.pallas_call(
        functools.partial(kernel, planes),
        out_shape=(
            jax.ShapeDtypeStruct(q.shape, low),
            jax.ShapeDtypeStruct(k.shape, low),
            jax.ShapeDtypeStruct(v.shape, low),
        ),
        in_specs=[any_space] * 5 + [vmem] * 2,
        out_specs=(any_space,) * 3,
        scratch_shapes=[
            pltpu.VMEM(o.shape, low),
            pltpu.VMEM(g.shape, low),
            pltpu.VMEM((span, wide), low),
            pltpu.VMEM((span, wide), low),
            pltpu.VMEM((window, D), low),
            pltpu.VMEM((window, D), low),
            pltpu.VMEM((D, window), low),
            pltpu.VMEM((8, span), jnp.int32),
            pltpu.VMEM((8, rows), jnp.int32),
            pltpu.VMEM((8, window), jnp.int32),
            pltpu.VMEM((2 * heads * PLANE, rows), wider),
            pltpu.VMEM((2 * heads, span), wider),
            pltpu.VMEM((window, D), wider),
            pltpu.VMEM((window, D), wider),
            pltpu.VMEM((span // BLOCK * D, heads * BLOCK), wider),
            pltpu.VMEM((span, wide), low),
            pltpu.VMEM((2, span, D), low),
            pltpu.VMEM((2, span, D), low),
            pltpu.VMEM((2, span, D), low),
            pltpu.VMEM((2, span, D), low),
            pltpu.VMEM((2, span, D), low),
            pltpu.VMEM((2, CHUNKS, PLANE_X - 1, rows, wide // CHUNKS), low),
            pltpu.VMEM((CHUNKS, PLANE_X - 1, rows, wide // CHUNKS), low),
            sems((2, CHUNKS, ROUTE_SEMS)),
            sems((2, CHUNKS, ROUTE_SEMS)),
            sems((CHUNKS, ROUTE_SEMS)),
            sems((CHUNKS, ROUTE_SEMS)),
            sems((4, PLANE - 1)),
            sems((4, PLANE - 1)),
            sems((2, PLANE - 1)),
            sems((2, PLANE - 1)),
            sems((10,)),
            sems((10,)),
            sems((8,)),
        ],
        compiler_params=pltpu.CompilerParams(
            collective_id=0, has_side_effects=True, vmem_limit_bytes=VMEM_LIMIT
        ),
        name="attention_back",
    )(q, g, o, k, v, segments[None, :], lse)
    return pl.pallas_call(
        hand_over,
        in_specs=[any_space] * 3,
        out_specs=[any_space] * 3,
        scratch_shapes=[pltpu.VMEM(x.shape, x.dtype) for x in grads] + [sems((3, PIECES)), sems((3, PIECES))],
        out_shape=[jax.ShapeDtypeStruct(x.shape, x.dtype) for x in grads],
        compiler_params=pltpu.CompilerParams(vmem_limit_bytes=VMEM_LIMIT),
        name="hand_over",
    )(*grads)


def solution(mesh):
    rows = P(("dp", "seq"), None)
    in_specs = (rows, rows, rows, rows, rows, P(None, ("dp", "seq")), P(("dp", "seq")))
    return jax.shard_map(
        on_device, mesh=mesh, in_specs=in_specs, out_specs=(rows, rows, rows), check_vma=False
    )
```

```python
import functools
import math

import jax
import jax.numpy as jnp
from jax import lax
from jax.experimental import pallas as pl
from jax.experimental.pallas import tpu as pltpu
from jax.sharding import PartitionSpec as P

D = 128
LOG2E = math.log2(math.e)
MESH = pl.DeviceIdType.MESH
PLANE = 8
PLANE_X = 4
HALO = 2
CHUNKS = 4
PIECES = 4
WHOLE = 2
ROUTE_SEMS = 10
BLOCK = 256
VMEM_LIMIT = 60 * 1024 * 1024


def dev(index):
    return {"seq": index}


def greet(me, plane, rank, planes, reach):
    barrier = pltpu.get_barrier_semaphore()
    for o in range(1, PLANE):
        peer = plane * PLANE + lax.rem(rank + o, PLANE)
        pl.semaphore_signal(barrier, inc=1, device_id=dev(peer), device_id_type=MESH)
    count = PLANE - 1
    for dz in range(1, reach + 1):
        up = plane + dz < planes
        down = plane >= dz

        @pl.when(up)
        def _():
            pl.semaphore_signal(barrier, inc=1, device_id=dev(me + dz * PLANE), device_id_type=MESH)

        @pl.when(down)
        def _():
            pl.semaphore_signal(barrier, inc=1, device_id=dev(me - dz * PLANE), device_id_type=MESH)

        count = count + up.astype(jnp.int32) + down.astype(jnp.int32)
    pl.semaphore_wait(barrier, count)


class Route:
    def __init__(self, x_first, plane, rank, source, target, stage, sems):
        self.x_first, self.plane = x_first, plane
        self.y, self.x = rank // PLANE_X, lax.rem(rank, PLANE_X)
        self.source, self.target, self.stage = source, target, stage
        self.send, self.recv = sems

    def rank(self, dy, dx):
        y = self.y if dy == 0 else 1 - self.y
        return y * PLANE_X + lax.rem(self.x + dx + PLANE_X, PLANE_X)

    def copy(self, n, source, target, peer):
        return pltpu.make_async_remote_copy(
            source, target, self.send.at[n], self.recv.at[n],
            device_id=dev(self.plane * PLANE + peer), device_id_type=MESH,
        )

    def first_leg(self, dx):
        peer = self.rank(0, dx) if self.x_first else self.rank(1, 0)
        return self.copy(dx - 1, self.source(self.rank(1, dx)), self.stage.at[dx - 1], peer)

    def second_leg(self, dx):
        if self.x_first:
            origin, peer = self.rank(0, -dx), self.rank(1, 0)
        else:
            origin, peer = self.rank(1, 0), self.rank(0, dx)
        return self.copy(2 + dx, self.stage.at[dx - 1], self.target(origin), peer)

    def straight(self, dx):
        peer = self.rank(0, dx) if dx else self.rank(1, 0)
        return self.copy(6 + dx, self.source(peer), self.target(self.rank(0, 0)), peer)

    def start_first(self):
        for dx in range(1, PLANE_X):
            self.first_leg(dx).start()

    def start_straight(self):
        for dx in range(PLANE_X):
            self.straight(dx).start()

    def pass_on(self):
        for dx in range(1, PLANE_X):
            self.first_leg(dx).wait_recv()
            self.second_leg(dx).start()

    def wait_arrivals(self):
        for dx in range(PLANE_X):
            origin = self.rank(0, -dx) if dx else self.rank(1, 0)
            self.copy(6 + dx, self.target(origin), self.target(origin), origin).wait_recv()
        for dx in range(1, PLANE_X):
            origin = self.rank(1, -dx)
            self.copy(2 + dx, self.target(origin), self.target(origin), origin).wait_recv()

    def wait_sends(self):
        for dx in range(1, PLANE_X):
            self.first_leg(dx).wait_send()
            self.second_leg(dx).wait_send()
        for dx in range(PLANE_X):
            self.straight(dx).wait_send()


def tile_terms(k_rows, v_rows, q_rows, g_rows, lse_row, delta_row, visible):
    nt = (((1,), (1,)), ((), ()))
    scores = lax.dot_general(k_rows, q_rows, nt, preferred_element_type=jnp.float32)
    weights = jnp.exp2(scores * (LOG2E / math.sqrt(D)) - lse_row)
    if visible is not None:
        weights = jnp.where(visible(), weights, 0.0)
    d_weights = lax.dot_general(v_rows, g_rows, nt, preferred_element_type=jnp.float32)
    dscore = (weights * (d_weights - delta_row)).astype(jnp.bfloat16)
    return weights.astype(jnp.bfloat16), dscore


def begins_at(ids, first):
    at = lax.broadcasted_iota(jnp.int32, ids.shape, 1)
    begins = (ids != pltpu.roll(ids, 1, 1)) & (at > first)
    found = jnp.where(begins, at, first)
    step = 1
    while step < ids.shape[1]:
        found = jnp.where(at >= step, jnp.maximum(found, pltpu.roll(found, step, 1)), found)
        step *= 2
    return found


def kernel(
    planes, q, g, o, k, v, seg, lse, grad_q, grad_k, grad_v,
    o_here, g_here, q_in, g_in, k_in, v_in, k_t, start, seg_here, seg_win, stats, stats_in,
    dk, dv, dq_t, dq_low, far_out, far_in, near_out, near_in, low, stage, stage_back,
    r_send, r_recv, b_send, b_recv, send, recv, kv_send, kv_recv, z_send, z_recv, local,
):
    rows = q.shape[0]
    span = rows * PLANE
    wide = q_in.shape[1]
    heads = wide // D
    me = lax.axis_index("seq")
    plane, rank = me // PLANE, lax.rem(me, PLANE)
    own = HALO * span
    blocks = span // BLOCK
    narrow = wide // CHUNKS
    per_chunk = narrow // D
    across = per_chunk * BLOCK
    inv_root = 1.0 / math.sqrt(D)

    def part(index, width):
        return pl.ds(pl.multiple_of(index * width, width), width)

    def own_part(s):
        return pl.ds(pl.multiple_of(own + s * rows, rows), rows)

    pieces = [
        (lambda p: seg_here, lambda s: seg_win.at[:, own_part(s)]),
        (lambda p: k.at[:, part(p, D)], lambda s: k_in.at[own_part(s), :]),
        (lambda p: v.at[:, part(p, D)], lambda s: v_in.at[own_part(s), :]),
        (lambda p: stats.at[part(p, 2 * heads), :], lambda s: stats_in.at[:, part(s, rows)]),
        (lambda p: q.at[:, part(p, wide)], lambda s: q_in.at[part(s, rows), :]),
        (lambda p: g.at[:, part(p, wide)], lambda s: g_in.at[part(s, rows), :]),
    ]
    last = 3

    def routes(c):
        made = []
        for n, (array, gathered) in enumerate(((q, q_in), (g, g_in))):
            def source(p, array=array):
                return array.at[:, pl.ds(pl.multiple_of(p * wide + c * narrow, narrow), narrow)]

            def target(s, gathered=gathered):
                return gathered.at[part(s, rows), part(c, narrow)]

            made.append(Route(
                n == 0, plane, rank, source, target, stage.at[n, c], (r_send.at[n, c], r_recv.at[n, c])
            ))
        return made

    def route_back(c):
        def source(p):
            return dq_low.at[part(p, rows), pl.ds(c * narrow, narrow)]

        def target(s):
            return grad_q.at[:, pl.ds(pl.multiple_of(s * wide + c * narrow, narrow), narrow)]

        return Route(c % 2 == 0, plane, rank, source, target, stage_back.at[c], (b_send.at[c], b_recv.at[c]))

    back = [route_back(c) for c in range(CHUNKS)]

    def own_copy(n):
        source, target = pieces[n]
        return pltpu.make_async_copy(source(rank), target(rank), local.at[n])

    def plane_copy(n, o):
        source, target = pieces[n]
        peer = lax.rem(rank + o, PLANE)
        return pltpu.make_async_remote_copy(
            source(peer), target(rank), send.at[n, o - 1], recv.at[n, o - 1],
            device_id=dev(plane * PLANE + peer), device_id_type=MESH,
        )

    def arrival(n, o):
        source, target = pieces[n]
        origin = lax.rem(rank + PLANE - o, PLANE)
        return pltpu.make_async_remote_copy(
            source(rank), target(origin), send.at[n, o - 1], recv.at[n, o - 1],
            device_id=dev(plane * PLANE + origin), device_id_type=MESH,
        )

    def kv_copy(n, o, origin):
        peer = lax.rem(rank + o, PLANE)
        return pltpu.make_async_remote_copy(
            low.at[n, part(peer, rows), :], (grad_k, grad_v)[n].at[:, part(origin, D)],
            kv_send.at[n, o - 1], kv_recv.at[n, o - 1],
            device_id=dev(plane * PLANE + peer), device_id_type=MESH,
        )

    def z_copy(n, source, target, planes_on):
        return pltpu.make_async_remote_copy(
            source, target, z_send.at[n], z_recv.at[n],
            device_id=dev(me + planes_on * PLANE), device_id_type=MESH,
        )

    def seg_copy(dz):
        return z_copy(dz - 1, seg_win.at[:, pl.ds(own, span)], seg_win.at[:, pl.ds(own - dz * span, span)], dz)

    def halo_copy(n, dz):
        win = (k_in, v_in)[n]
        held, there = pl.ds(own - (dz - 1) * span, span), pl.ds(own - dz * span, span)
        return z_copy(2 * dz + n, win.at[held, :], win.at[there, :], 1)

    def far_copy(n):
        return z_copy(6 + n, far_out.at[n], far_in.at[n], -1)

    def near_copy(n):
        return z_copy(8 + n, near_out.at[n], near_in.at[n], -1)

    def start_chunk(c):
        for path in routes(c):
            path.start_first()
        for path in routes(c):
            path.start_straight()

    def pass_on(c):
        for path in routes(c):
            path.pass_on()

    def start_back(c):
        back[c].start_first()
        back[c].start_straight()

    def transpose_keys(dz):
        held = pl.ds(own - dz * span, span)
        k_t[:, held] = k_in[held, :].T

    def take_halo(dz):
        held = pl.ds(own - dz * span, span)

        @pl.when(plane >= dz)
        def _():
            for n in range(2):
                halo_copy(n, dz).wait_recv()

        @pl.when(plane < dz)
        def _():
            k_in[held, :] = jnp.zeros((span, D), k_in.dtype)
            v_in[held, :] = jnp.zeros((span, D), v_in.dtype)

        if dz < HALO:
            @pl.when((plane >= dz) & (plane + 1 < planes))
            def _():
                for n in range(2):
                    halo_copy(n, dz + 1).start()
        transpose_keys(dz)

    def tiles(c, dz, first):
        operands = []
        for i in range(blocks):
            here = pl.ds(i * BLOCK, BLOCK)

            def stacked(ref, here=here):
                return jnp.concatenate(
                    [ref[here, pl.ds(pl.multiple_of(c * narrow + h * D, D), D)] for h in range(per_chunk)], axis=0
                )

            def in_line(at, here=here):
                return jnp.concatenate(
                    [stats_in[pl.ds(at + c * per_chunk + h, 1), here] for h in range(per_chunk)], axis=1
                )

            start_row = jnp.concatenate([start[0:1, here]] * per_chunk, axis=1)
            operands.append((stacked(q_in), stacked(g_in), in_line(0) * LOG2E, in_line(heads), start_row))
        totals = [None] * blocks
        down = lax.broadcasted_iota(jnp.int32, (BLOCK, across), 0)
        query_at = lax.rem(lax.broadcasted_iota(jnp.int32, (1, across), 1), BLOCK)
        for before in range(HALO * blocks + 1):
            for i in range(blocks):
                j = HALO * blocks + i - before
                if j // blocks != HALO - dz:
                    continue
                there = pl.ds(j * BLOCK, BLOCK)
                q_rows, g_rows, lse_row, delta_row, start_row = operands[i]

                def visible(j=j, before=before, start_row=start_row):
                    seen = down >= start_row - j * BLOCK
                    return seen & (down <= query_at) if before == 0 else seen

                weights, dscore = tile_terms(
                    k_in[there, :], v_in[there, :], q_rows, g_rows, lse_row, delta_row, visible
                )
                dv[there, :] += jnp.dot(weights, g_rows, preferred_element_type=jnp.float32)
                dk[there, :] += jnp.dot(dscore, q_rows, preferred_element_type=jnp.float32)
                term = jnp.dot(k_t[:, there], dscore, preferred_element_type=jnp.float32)
                totals[i] = term if totals[i] is None else totals[i] + term
        for i in range(blocks):
            if first:
                dq_t[pl.ds(i * D, D), part(c, across)] = totals[i]
            else:
                dq_t[pl.ds(i * D, D), part(c, across)] += totals[i]

    def finish_queries(c):
        for i in range(blocks):
            for h in range(per_chunk):
                total = dq_t[pl.ds(i * D, D), pl.ds(pl.multiple_of(c * across + h * BLOCK, BLOCK), BLOCK)]
                dq_low[pl.ds(i * BLOCK, BLOCK), pl.ds(pl.multiple_of(c * narrow + h * D, D), D)] = (
                    total.T * inv_root
                ).astype(dq_low.dtype)

    load_o = pltpu.make_async_copy(o, o_here, local.at[6])
    load_g = pltpu.make_async_copy(g, g_here, local.at[7])
    load_o.start()
    load_g.start()
    seg_here[...] = jnp.broadcast_to(seg[...], seg_here.shape)
    greet(me, plane, rank, planes, HALO)
    for n in range(last):
        if n == 1:
            for path in routes(0):
                path.start_first()
        for o_at in range(1, PLANE):
            plane_copy(n, o_at).start()
        own_copy(n).start()
    for path in routes(0):
        path.start_straight()
    own_copy(4).start()
    own_copy(5).start()
    for n in range(last):
        own_copy(n).wait()
        for o_at in range(1, PLANE):
            arrival(n, o_at).wait_recv()
        if n == 0:
            for dz in range(1, HALO + 1):
                @pl.when(plane + dz < planes)
                def _():
                    seg_copy(dz).start()
            pass_on(0)
        else:
            @pl.when(plane + 1 < planes)
            def _():
                halo_copy(n - 1, 1).start()

    load_o.wait()
    load_g.wait()

    @pl.loop(0, PLANE)
    def _(p):
        sums = []
        for h in range(heads):
            features = pl.ds(pl.multiple_of(p * wide + h * D, D), D)
            product = o_here[:, features].astype(jnp.float32) * g_here[:, features].astype(jnp.float32)
            sums.append(jnp.sum(product.T, axis=0, keepdims=True))
        stats[part(p * 2, heads), :] = lse[part(p, heads), :]
        stats[part(p * 2 + 1, heads), :] = jnp.concatenate(sums, axis=0)

    for o_at in range(1, PLANE):
        plane_copy(last, o_at).start()
    own_copy(last).start()
    start_chunk(1)
    dk[...] = jnp.zeros_like(dk)
    dv[...] = jnp.zeros_like(dv)
    transpose_keys(0)
    for dz in range(1, HALO + 1):
        @pl.when(plane >= dz)
        def _():
            seg_copy(dz).wait_recv()
    start[...] = begins_at(seg_win[...], own - jnp.minimum(plane, HALO) * span)[:, own:]
    own_copy(last).wait()
    own_copy(4).wait()
    own_copy(5).wait()
    for o_at in range(1, PLANE):
        arrival(last, o_at).wait_recv()

    @pl.loop(0, WHOLE)
    def _(c):
        for path in routes(c):
            path.wait_arrivals()
        for dz in range(HALO + 1):
            if dz > 0:
                @pl.when(c == 0)
                def _():
                    take_halo(dz)

            tiles(c, dz, dz == 0)
            if dz == 0:
                pass_on(c + 1)
                start_chunk(c + 2)
            if dz == 1:
                @pl.when(c == WHOLE - 1)
                def _():
                    pass_on(WHOLE + 1)
                    back[0].pass_on()

        finish_queries(c)
        for n in range(WHOLE):
            @pl.when(c == n)
            def _():
                start_back(n)

    @pl.loop(WHOLE, CHUNKS)
    def _(c):
        for path in routes(c):
            path.wait_arrivals()
        tiles(c, 2, True)

    far_out[0] = (dk[:span, :] * inv_root).astype(far_out.dtype)
    far_out[1] = dv[:span, :].astype(far_out.dtype)

    @pl.when(plane >= 2)
    def _():
        for n in range(2):
            far_copy(n).start()

    back[1].pass_on()

    @pl.loop(WHOLE, CHUNKS)
    def _(c):
        tiles(c, 1, False)

    dk[pl.ds(span, span), :] = dk[pl.ds(span, span), :] * inv_root
    takes_far = (plane >= 1) & (plane + 1 < planes)

    @pl.when(takes_far)
    def _():
        for n in range(2):
            far_copy(n).wait_recv()
            total = (dk, dv)[n]
            near_out[n] = (total[pl.ds(span, span), :] + far_in[n].astype(jnp.float32)).astype(near_out.dtype)

    @pl.when(plane + 1 >= planes)
    def _():
        for n in range(2):
            near_out[n] = (dk, dv)[n][pl.ds(span, span), :].astype(near_out.dtype)

    @pl.when(plane >= 1)
    def _():
        for n in range(2):
            near_copy(n).start()

    for c in range(WHOLE, CHUNKS):
        tiles(c, 0, False)
        if c > WHOLE:
            back[c - 1].pass_on()
        finish_queries(c)
        start_back(c)

    dk[pl.ds(own, span), :] = dk[pl.ds(own, span), :] * inv_root
    own_back = pltpu.make_async_copy(dq_low.at[part(rank, rows), :], grad_q.at[:, part(rank, wide)], local.at[4])
    own_back.start()
    own_kv = []
    for n in range(2):
        total = (dk, dv)[n]

        @pl.when(plane + 1 < planes)
        def _():
            near_copy(n).wait_recv()
            low[n] = (total[pl.ds(own, span), :] + near_in[n].astype(jnp.float32)).astype(low.dtype)

        @pl.when(plane + 1 >= planes)
        def _():
            low[n] = total[pl.ds(own, span), :].astype(low.dtype)

        for o_at in range(1, PLANE):
            kv_copy(n, o_at, rank).start()
        own_kv.append(pltpu.make_async_copy(
            low.at[n, part(rank, rows), :], (grad_k, grad_v)[n].at[:, part(rank, D)], local.at[6 + n]
        ))
        own_kv[n].start()
    for c in range(WHOLE + 1, CHUNKS):
        back[c].pass_on()

    own_back.wait()
    for n in range(2):
        own_kv[n].wait()
    for c in range(CHUNKS):
        for path in routes(c):
            path.wait_sends()
        back[c].wait_arrivals()
        back[c].wait_sends()
    for o_at in range(1, PLANE):
        for n in range(last + 1):
            plane_copy(n, o_at).wait_send()
        origin = lax.rem(rank + PLANE - o_at, PLANE)
        for n in range(2):
            kv_copy(n, o_at, origin).wait()
    for dz in range(1, HALO + 1):
        @pl.when(plane + dz < planes)
        def _():
            seg_copy(dz).wait_send()

        @pl.when((plane + 1 < planes) & (plane + 1 >= dz))
        def _():
            for n in range(2):
                halo_copy(n, dz).wait_send()

    @pl.when(plane >= 2)
    def _():
        for n in range(2):
            far_copy(n).wait_send()

    @pl.when(plane >= 1)
    def _():
        for n in range(2):
            near_copy(n).wait_send()


def hand_over(*refs):
    sources, targets, held, arrived, left = refs[:3], refs[3:6], refs[6:9], refs[9], refs[10]
    copies = []
    for n in range(3):
        rows = sources[n].shape[0] // PIECES
        for m in range(PIECES):
            at = pl.ds(m * rows, rows)
            copies.append((
                pltpu.make_async_copy(sources[n].at[at, :], held[n].at[at, :], arrived.at[n, m]),
                pltpu.make_async_copy(held[n].at[at, :], targets[n].at[at, :], left.at[n, m]),
            ))
    for load, _ in copies:
        load.start()
    for load, store in copies:
        load.wait()
        store.start()
    for _, store in copies:
        store.wait()


def on_device(q, k, v, o, g, lse, segments):
    planes = lax.axis_size("seq") // PLANE
    rows = q.shape[0]
    span = rows * PLANE
    heads = lse.shape[0] // PLANE
    wide = heads * D
    window = (HALO + 1) * span
    any_space = pl.BlockSpec(memory_space=pl.ANY)
    vmem = pl.BlockSpec(memory_space=pltpu.VMEM)
    low, wider, sems = jnp.bfloat16, jnp.float32, pltpu.SemaphoreType.DMA
    grads = pl.pallas_call(
        functools.partial(kernel, planes),
        out_shape=(
            jax.ShapeDtypeStruct(q.shape, low),
            jax.ShapeDtypeStruct(k.shape, low),
            jax.ShapeDtypeStruct(v.shape, low),
        ),
        in_specs=[any_space] * 5 + [vmem] * 2,
        out_specs=(any_space,) * 3,
        scratch_shapes=[
            pltpu.VMEM(o.shape, low),
            pltpu.VMEM(g.shape, low),
            pltpu.VMEM((span, wide), low),
            pltpu.VMEM((span, wide), low),
            pltpu.VMEM((window, D), low),
            pltpu.VMEM((window, D), low),
            pltpu.VMEM((D, window), low),
            pltpu.VMEM((8, span), jnp.int32),
            pltpu.VMEM((8, rows), jnp.int32),
            pltpu.VMEM((8, window), jnp.int32),
            pltpu.VMEM((2 * heads * PLANE, rows), wider),
            pltpu.VMEM((2 * heads, span), wider),
            pltpu.VMEM((window, D), wider),
            pltpu.VMEM((window, D), wider),
            pltpu.VMEM((span // BLOCK * D, heads * BLOCK), wider),
            pltpu.VMEM((span, wide), low),
            pltpu.VMEM((2, span, D), low),
            pltpu.VMEM((2, span, D), low),
            pltpu.VMEM((2, span, D), low),
            pltpu.VMEM((2, span, D), low),
            pltpu.VMEM((2, span, D), low),
            pltpu.VMEM((2, CHUNKS, PLANE_X - 1, rows, wide // CHUNKS), low),
            pltpu.VMEM((CHUNKS, PLANE_X - 1, rows, wide // CHUNKS), low),
            sems((2, CHUNKS, ROUTE_SEMS)),
            sems((2, CHUNKS, ROUTE_SEMS)),
            sems((CHUNKS, ROUTE_SEMS)),
            sems((CHUNKS, ROUTE_SEMS)),
            sems((4, PLANE - 1)),
            sems((4, PLANE - 1)),
            sems((2, PLANE - 1)),
            sems((2, PLANE - 1)),
            sems((10,)),
            sems((10,)),
            sems((8,)),
        ],
        compiler_params=pltpu.CompilerParams(
            collective_id=0, has_side_effects=True, vmem_limit_bytes=VMEM_LIMIT
        ),
        name="attention_back",
    )(q, g, o, k, v, segments[None, :], lse)
    return pl.pallas_call(
        hand_over,
        in_specs=[any_space] * 3,
        out_specs=[any_space] * 3,
        scratch_shapes=[pltpu.VMEM(x.shape, x.dtype) for x in grads] + [sems((3, PIECES)), sems((3, PIECES))],
        out_shape=[jax.ShapeDtypeStruct(x.shape, x.dtype) for x in grads],
        compiler_params=pltpu.CompilerParams(vmem_limit_bytes=VMEM_LIMIT),
        name="hand_over",
    )(*grads)


def solution(mesh):
    rows = P(("dp", "seq"), None)
    in_specs = (rows, rows, rows, rows, rows, P(None, ("dp", "seq")), P(("dp", "seq")))
    return jax.shard_map(
        on_device, mesh=mesh, in_specs=in_specs, out_specs=(rows, rows, rows), check_vma=False
    )
```
